32 devices in a mesh: wide: 4 (over y, x), narrow: 8 (over z, core).
Axes of the slice: x: 2, y: 2, z: 4, core: 2. Of those that a mesh axis runs over, the one named last changes fastest.
Arguments:
- saved_inputs: bfloat16 [3, 8192, 4096], P(None, 'wide', 'narrow'), may hold values from -6 to 6
- cotangent: bfloat16 [8192, 4096], P('wide', 'narrow'), may hold values from -6 to 6
- w_self: bfloat16 [3, 4096, 512], P(None, 'narrow'), may hold values from -0.1875 to 0.1875
- w_cross: bfloat16 [3, 4096, 512], P(None, 'narrow'), may hold values from -0.1875 to 0.1875
Outputs:
- grad_in: bfloat16 [8192, 4096], P('wide', 'narrow')
- grad_self: float32 [3, 4096, 512], P(None, ('narrow', 'wide'))
- grad_cross: float32 [3, 4096, 512], P(None, ('narrow', 'wide'))
The draws below stay inside these ranges and needn't reach their ends.
All inputs are finite; a program needn't handle non-finite values.
Results may differ from the reference program's by a relative error of at most 0.0057.
Values may be sent and summed in bfloat16 or wider, within the bound.
No kernel may reach another device: no remote copies, remote signals or barrier semaphores. Data moves between devices by JAX's collectives and lax.ppermute only.
A program may use at most 128 MiB of HBM per device.

```python
import math
import jax
import jax.numpy as jnp
import numpy as np

BLK = 512
LEVELS = 3
D = 4096
TOKENS = 8192


def spiked(result, stream_key, source, target, parts, factor):
    def block_of(dim):
        return (jnp.arange(result.shape[dim]) // (result.shape[dim] // parts)).reshape((-1,) + (1,) * (result.ndim - 1 - dim))

    one_side = jax.random.permutation(stream_key, parts)[block_of(target)]
    second = (block_of(target) + parts // 2) % parts
    return jnp.where((block_of(source) == one_side) | (block_of(source) == second), factor * result, result)


def block_levels(stream_key, extent, cuts, smallest, top_value):
    level, own = 1.0, jax.random.fold_in(stream_key, 6)
    for position, parts in cuts:
        draws = jnp.exp(jax.random.uniform(jax.random.fold_in(own, position), (parts,), jnp.float32, smallest / len(cuts), top_value / len(cuts)))
        level = level * jnp.repeat(draws, extent[position] // parts).reshape([-1 if axis == position else 1 for axis in range(len(extent))])
    return level


def centred(key, dims, deviation, most, shards=(), dtype=jnp.bfloat16):
    drawn = deviation * jax.random.normal(key, dims, jnp.float32)
    if shards:
        drawn = drawn * block_levels(key, dims, shards, -0.22, 0.18)
    return jnp.clip(drawn, -most, most).astype(dtype)


def bell_draw_with(rng, extent, deviation, limit, shards, heavy, dtype=jnp.bfloat16):
    drawn = deviation * jax.random.normal(rng, extent, jnp.float32)
    if shards:
        drawn = drawn * block_levels(rng, extent, shards, -0.22, 0.18)
    return jnp.clip(spiked(drawn, jax.random.fold_in(rng, 3), *heavy), -limit, limit).astype(dtype)


def setup_inputs(seed: int = 0) -> dict:
    key_of = jax.random.split(jax.random.key(seed), 5)
    saved_inputs = bell_draw_with(key_of[0], (LEVELS, TOKENS, D), 1.0, 6.0, ((1, 4), (2, 8)), (1, 2, 8, 2.0))
    cotangent = centred(key_of[1], (TOKENS, D), 1.0, 6.0, ((0, 4), (1, 8)))
    w_self = centred(key_of[2], (LEVELS, D, BLK), (2 * BLK) ** -0.5, 0.1875, ((1, 8),))
    w_cross = centred(key_of[3], (LEVELS, D, BLK), (2 * BLK) ** -0.5, 0.1875, ((1, 8),))
    return dict(saved_inputs=saved_inputs, cotangent=cotangent, w_self=w_self, w_cross=w_cross)


def reference(saved_inputs, cotangent, w_self, w_cross):
    blocks = D // BLK
    scale = 1.0 / math.sqrt(TOKENS)
    grad = cotangent.reshape(TOKENS, blocks, BLK)
    self_list = [None] * LEVELS
    cross_list = [None] * LEVELS
    for level in reversed(range(LEVELS)):
        partner = np.arange(blocks) ^ 1 << level
        inputs = saved_inputs[level].reshape(TOKENS, blocks, BLK).astype(jnp.float32)
        gflt = grad.astype(jnp.float32)
        a_blocks = w_self[level].reshape(blocks, BLK, BLK).astype(jnp.float32)
        c_blocks = w_cross[level].reshape(blocks, BLK, BLK).astype(jnp.float32)
        self_list[level] = (jnp.einsum('tnk,tnj->nkj', inputs, gflt) * scale).reshape(D, BLK)
        cross_list[level] = (jnp.einsum('tnk,tnj->nkj', inputs[:, partner], gflt) * scale).reshape(D, BLK)
        own = jnp.einsum('tnj,nkj->tnk', gflt, a_blocks)
        far = jnp.einsum('tnj,nkj->tnk', gflt[:, partner], c_blocks[partner])
        grad = (own + far).astype(jnp.bfloat16)
    return (grad.reshape(TOKENS, D), jnp.stack(self_list), jnp.stack(cross_list))
```

```python
import math

import jax
import jax.numpy as jnp
from jax import lax
from jax.experimental import pallas as pl
from jax.experimental.pallas import tpu as pltpu
from jax.sharding import PartitionSpec as P

LEVELS = 3
CUTS = (3, 3, 3, 3, 2, 2)
GROUPS = ((0, 1, 2), (3, 4), (5,))
ROW_TILE = 16
WINDOW = 2
VMEM_LIMIT = 40 * 1024 * 1024

ANY = pl.BlockSpec(memory_space=pl.ANY)
WHOLE = pl.BlockSpec(memory_space=pltpu.VMEM)


def swap(array, axis, mask):
    return lax.ppermute(array, axis, [(i, i ^ mask) for i in range(lax.axis_size(axis))])


def outer_sum(left, right):
    return lax.dot_general(
        left, right, (((0,), (0,)), ((), ())), preferred_element_type=jnp.float32
    )


def times_trans(left, right):
    return lax.dot_general(
        left, right, (((1,), (1,)), ((), ())), preferred_element_type=jnp.float32
    )


def params():
    return pltpu.CompilerParams(vmem_limit_bytes=VMEM_LIMIT)


def cost(flops, nbytes):
    return pl.CostEstimate(flops=flops, bytes_accessed=nbytes, transcendentals=0)


def row_cuts(tokens):
    unit = tokens // sum(CUTS)
    assert unit % ROW_TILE == 0
    cuts, start = [], 0
    for c in CUTS:
        cuts.append((start, c * unit))
        start += c * unit
    return cuts


def next_grad(grad, far, w_self, far_cross, level, deps=(), fetch=None):
    size, width = grad.shape
    n_in = 4 + len(deps)

    def body(*refs):
        grad_ref, far_ref, a_ref, c_ref = refs[:4]
        if fetch is None:
            out_ref = refs[n_in]
        else:
            src_ref, out_ref, cut_ref, sem = refs[n_in:]
            copy = pltpu.make_async_copy(
                src_ref.at[pl.ds(fetch[1], fetch[2])], cut_ref, sem
            )
            copy.start()
        total = times_trans(grad_ref[...], a_ref[0]) + times_trans(far_ref[...], c_ref[...])
        out_ref[...] = total.astype(jnp.bfloat16)
        if fetch is not None:
            copy.wait()

    weight = pl.BlockSpec((1,) + w_self.shape[1:], lambda i: (level, 0, 0))
    operands = [grad, far, w_self, far_cross, *deps]
    in_specs = [WHOLE, WHOLE, weight, WHOLE] + [ANY] * len(deps)
    out_shape = [jax.ShapeDtypeStruct((size, width), jnp.bfloat16)]
    scratch = []
    if fetch is not None:
        operands.append(fetch[0])
        in_specs.append(ANY)
        out_shape.append(jax.ShapeDtypeStruct((fetch[2], width), jnp.bfloat16))
        scratch.append(pltpu.SemaphoreType.DMA)
    out = pl.pallas_call(
        body,
        grid=(1,),
        out_shape=out_shape,
        in_specs=in_specs,
        out_specs=[WHOLE] * len(out_shape),
        scratch_shapes=scratch,
        compiler_params=params(),
        cost_estimate=cost(4 * size * width * width, 6 * size * width + 4 * width * width),
        name=f"next_grad_{level}",
    )(*operands)
    return out if fetch is not None else out[0]


def weight_sums(saved_inputs, level, start, grads, fars, before, scale, last, deps=()):
    sizes = [g.shape[0] for g in grads]
    rows, width = sum(sizes), saved_inputs.shape[2]
    blk = grads[0].shape[1]
    parts = lax.axis_size("wide")
    share = width // parts
    m = len(grads)
    n_before = 0 if before is None else 1

    def body(*refs):
        x_ref = refs[0]
        g_refs, f_refs = refs[1 : 1 + m], refs[1 + m : 1 + 2 * m]
        pos = 1 + 2 * m
        old = refs[pos] if n_before else None
        pos += n_before + len(deps)
        n_out = parts if last else 1
        outs = refs[pos : pos + n_out]
        scratch = refs[pos + n_out :]
        x_buf, sem = scratch[0], scratch[1]
        total = scratch[2] if last else outs[0]
        copy = pltpu.make_async_copy(x_ref.at[level, pl.ds(start, rows)], x_buf, sem)
        copy.start()
        copy.wait()
        for which, sides in enumerate((g_refs, f_refs)):
            at = 0
            acc = old[which] if n_before else None
            for size, side in zip(sizes, sides):
                term = outer_sum(x_buf[at : at + size], side[...])
                acc = term if acc is None else acc + term
                at += size
            total[which] = acc * scale if last else acc
        if last:
            me = lax.axis_index("wide")
            outs[0][...] = total[:, pl.ds(pl.multiple_of(me * share, share), share)]
            for k in range(1, parts):
                there = pl.multiple_of((me ^ k) * share, share)
                outs[k][...] = total[:, pl.ds(there, share)].astype(jnp.bfloat16)

    sums = jax.ShapeDtypeStruct((2, width, blk), jnp.float32)
    if last:
        out_shape = [jax.ShapeDtypeStruct((2, share, blk), jnp.float32)]
        out_shape += [jax.ShapeDtypeStruct((2, share, blk), jnp.bfloat16)] * (parts - 1)
    else:
        out_shape = [sums]
    scratch = [pltpu.VMEM((rows, width), saved_inputs.dtype), pltpu.SemaphoreType.DMA]
    if last:
        scratch.append(pltpu.VMEM(sums.shape, jnp.float32))
    operands = [saved_inputs, *grads, *fars] + ([before] if n_before else []) + list(deps)
    out = pl.pallas_call(
        body,
        grid=(1,),
        out_shape=out_shape,
        in_specs=[ANY] + [WHOLE] * (2 * m + n_before) + [ANY] * len(deps),
        out_specs=[WHOLE] * len(out_shape),
        scratch_shapes=scratch,
        compiler_params=params(),
        cost_estimate=cost(4 * rows * width * blk, 6 * rows * width + 16 * width * blk),
        name=f"weight_sums_{level}",
    )(*operands)
    return out if last else out[0]


def far_blocks(w_cross):
    parts = lax.axis_size("wide")
    rows = w_cross.shape[1] // parts
    me = lax.axis_index("wide")
    out = [None] * LEVELS
    for level in reversed(range(LEVELS)):
        share = lax.dynamic_slice_in_dim(w_cross[level], me * rows, rows, 0)
        share = swap(share, "narrow", 1 << level)
        block = lax.dynamic_update_slice_in_dim(jnp.zeros_like(w_cross[level]), share, me * rows, 0)
        for k in range(1, parts):
            block = lax.dynamic_update_slice_in_dim(block, swap(share, "wide", k), (me ^ k) * rows, 0)
        out[level] = block
    return out


def wide_sum(kept, *terms):
    for k, term in enumerate(terms, 1):
        kept = kept + swap(term, "wide", k).astype(jnp.float32)
    return kept


def local(saved_inputs, cotangent, w_self, w_cross):
    tokens = saved_inputs.shape[1]
    scale = 1.0 / math.sqrt(tokens * lax.axis_size("wide"))
    cuts = row_cuts(tokens)
    blocks = far_blocks(w_cross)
    n = len(cuts)
    near = [[None] * n for _ in range(LEVELS + 1)]
    far = [[None] * n for _ in range(LEVELS)]
    top = LEVELS - 1
    for k in range(min(WINDOW, n)):
        near[top][k] = cotangent[cuts[k][0] : cuts[k][0] + cuts[k][1]]
        far[top][k] = swap(near[top][k], "narrow", 1 << top)
    for t in range(n + top):
        for level in reversed(range(LEVELS)):
            k = t - (top - level)
            if not 0 <= k < n:
                continue
            ahead = k + WINDOW
            fetch = None
            if level == top and ahead < n:
                fetch = (cotangent, *cuts[ahead])
            if far[level][k] is None:
                far[level][k] = swap(near[level][k], "narrow", 1 << level)
            out = next_grad(near[level][k], far[level][k], w_self, blocks[level], level, (), fetch)
            if fetch is not None:
                out, near[top][ahead] = out
                far[top][ahead] = swap(near[top][ahead], "narrow", 1 << top)
            near[level - 1][k] = out
    grad_self, grad_cross = [None] * LEVELS, [None] * LEVELS
    for level in reversed(range(LEVELS)):
        sums = None
        for group in GROUPS:
            last = group is GROUPS[-1]
            sums = weight_sums(
                saved_inputs,
                level,
                cuts[group[0]][0],
                [near[level][k] for k in group],
                [far[level][k] for k in group],
                sums,
                scale,
                last,
            )
        both = wide_sum(*sums)
        grad_self[level] = both[0]
        grad_cross[level] = swap(both[1].astype(jnp.bfloat16), "narrow", 1 << level)
    return (
        jnp.concatenate(near[-1]),
        jnp.stack(grad_self),
        jnp.stack(grad_cross).astype(jnp.float32),
    )


def solution(mesh):
    in_specs = (
        P(None, "wide", "narrow"),
        P("wide", "narrow"),
        P(None, "narrow", None),
        P(None, "narrow", None),
    )
    out_specs = (
        P("wide", "narrow"),
        P(None, ("narrow", "wide"), None),
        P(None, ("narrow", "wide"), None),
    )
    return jax.shard_map(local, mesh=mesh, in_specs=in_specs, out_specs=out_specs, check_vma=False)
```

```python
import math

import jax
import jax.numpy as jnp
from jax import lax
from jax.experimental import pallas as pl
from jax.experimental.pallas import tpu as pltpu
from jax.sharding import PartitionSpec as P

LEVELS = 3
TOP = LEVELS - 1
CUTS = (3, 6, 6, 7, 6, 4)
ROW_TILE = 16
VMEM_LIMIT = 24 * 1024 * 1024
WHOLE_VMEM = 60 * 1024 * 1024

ANY = pl.BlockSpec(memory_space=pl.ANY)
WHOLE = pl.BlockSpec(memory_space=pltpu.VMEM)
TOKEN = jax.ShapeDtypeStruct((8, 128), jnp.float32)


def in_hbm(array):
    return pltpu.with_memory_space_constraint(array, pltpu.HBM)


def swap(array, axis, mask):
    return lax.ppermute(array, axis, [(i, i ^ mask) for i in range(lax.axis_size(axis))])


def swap_both(array, wide_mask, narrow_mask):
    wide, narrow = lax.axis_size("wide"), lax.axis_size("narrow")
    pairs = [
        (w * narrow + i, (w ^ wide_mask) * narrow + (i ^ narrow_mask))
        for w in range(wide)
        for i in range(narrow)
    ]
    return lax.ppermute(array, ("wide", "narrow"), pairs)


def outer_sum(left, right):
    return lax.dot_general(
        left, right, (((0,), (0,)), ((), ())), preferred_element_type=jnp.float32
    )


def times_trans(left, right):
    return lax.dot_general(
        left, right, (((1,), (1,)), ((), ())), preferred_element_type=jnp.float32
    )


class Chain:
    def __init__(self):
        self.token = None

    def __call__(self, body, name, operands, in_specs, out_shape, out_specs, scratch=(), aliases=None, limit=VMEM_LIMIT, grid=1):
        n_in, n_out = len(operands), len(out_shape)
        held = [] if self.token is None else [self.token]

        def whole(*refs):
            ins = refs[:n_in]
            rest = refs[n_in + len(held) :]
            body(*ins, *rest[:n_out], *rest[n_out + 1 :])

        *outs, self.token = pl.pallas_call(
            whole,
            grid=(grid,),
            out_shape=[*out_shape, TOKEN],
            in_specs=[*in_specs] + [ANY] * len(held),
            out_specs=[*out_specs, ANY],
            scratch_shapes=list(scratch),
            input_output_aliases=aliases or {},
            compiler_params=pltpu.CompilerParams(vmem_limit_bytes=limit),
            name=name,
        )(*operands, *held)
        return outs


def row_cuts(tokens):
    unit = tokens // sum(CUTS)
    assert unit * sum(CUTS) == tokens and unit % ROW_TILE == 0
    cuts, start = [], 0
    for c in CUTS:
        cuts.append((start, c * unit))
        start += c * unit
    return cuts


def cut_out(chain, blocks, name, limit=WHOLE_VMEM):
    flat = [piece for block in blocks for piece in block]
    n = len(flat)

    def body(*refs):
        copies = []
        for b, block in enumerate(blocks):
            at = 0
            for _, where, size in block:
                j = len(copies)
                target = refs[n + b].at[pl.ds(at, size)]
                copy = pltpu.make_async_copy(where(refs[j], size), target, refs[-1].at[j])
                copy.start()
                copies.append(copy)
                at += size
        for copy in copies:
            copy.wait()

    return chain(
        body,
        name,
        [piece[0] for piece in flat],
        [ANY] * n,
        [
            jax.ShapeDtypeStruct((sum(p[2] for p in block), block[0][0].shape[-1]), block[0][0].dtype)
            for block in blocks
        ],
        [WHOLE] * len(blocks),
        [pltpu.SemaphoreType.DMA((n,))],
        limit=limit,
    )


def rows_at(start):
    return lambda ref, size: ref.at[pl.ds(start, size)]


def block_of(level):
    return lambda ref, size: ref.at[level]


def my_share(level, parts):
    def where(ref, size):
        first = pl.multiple_of(lax.axis_index("wide") % parts * size, size)
        return ref.at[level, pl.ds(first, size)]

    return where


def place_of(mask, parts):
    return lambda: (lax.axis_index("wide") ^ mask) % parts


def join_shares(chain, blocks, name):
    flat = [piece for block in blocks for piece in block]

    def body(*refs):
        ins, outs = list(refs[: len(flat)]), refs[len(flat) :]
        for out, block in zip(outs, blocks):
            for share, place in block:
                size = share.shape[0]
                out[pl.ds(pl.multiple_of(place() * size, size), size)] = ins.pop(0)[...]

    return chain(
        body,
        name,
        [share for share, _ in flat],
        [WHOLE] * len(flat),
        [
            jax.ShapeDtypeStruct((sum(a.shape[0] for a, _ in block),) + block[0][0].shape[1:], block[0][0].dtype)
            for block in blocks
        ],
        [WHOLE] * len(blocks),
    )


def next_grads(chain, w_self, jobs, name, into=None, halve=False, fetch=None, deps=()):
    width = w_self.shape[2]
    operands, in_specs, out_shape, out_specs, scratch, aliases = [], [], [], [], [], {}
    for level, grad, far, far_cross in jobs:
        operands += [w_self, far_cross, grad, far]
        in_specs += [weight_block(w_self, level), WHOLE, WHOLE, WHOLE]
    rows = [job[1].shape[0] for job in jobs]
    pieces = [size for size, job in zip(rows, jobs) if job[0] != 1]
    if halve:
        pieces = [rows[0] // 2] * 2
    for size in pieces:
        out_shape.append(jax.ShapeDtypeStruct((size, width), jnp.bfloat16))
        out_specs.append(WHOLE)
    operands += deps
    in_specs += [ANY] * len(deps)
    if into is not None:
        if not isinstance(into[0], jax.ShapeDtypeStruct):
            aliases[len(operands)] = len(out_shape)
            operands.append(in_hbm(into[0]))
            in_specs.append(ANY)
        out_shape.append(jax.ShapeDtypeStruct(into[0].shape, into[0].dtype))
        out_specs.append(ANY)
        stored = sum(size for size, job in zip(rows, jobs) if job[0] == 1)
        scratch += [pltpu.VMEM((stored, width), jnp.bfloat16), pltpu.SemaphoreType.DMA]
    if fetch is not None:
        operands.append(fetch[0])
        in_specs.append(ANY)
        out_shape.append(jax.ShapeDtypeStruct((fetch[2], fetch[0].shape[1]), fetch[0].dtype))
        out_specs.append(WHOLE)
        scratch.append(pltpu.SemaphoreType.DMA)

    def body(*refs):
        ins, outs = refs[: len(operands)], refs[len(operands) :]
        outs, scr = outs[: len(out_shape)], outs[len(out_shape) :]
        if fetch is not None:
            cut = pltpu.make_async_copy(ins[-1].at[pl.ds(*fetch[1:])], outs[-1], scr[-1])
            cut.start()
        at = 0
        for j in range(len(jobs)):
            a_ref, c_ref, grad_ref, far_ref = ins[4 * j : 4 * j + 4]
            total = times_trans(grad_ref[...], a_ref[0]) + times_trans(far_ref[...], c_ref[...])
            total = total.astype(jnp.bfloat16)
            if jobs[j][0] == 1:
                scr[0][at : at + rows[j]] = total
                at += rows[j]
            elif halve:
                outs[0][...] = total[: pieces[0]]
                outs[1][...] = total[pieces[0] :]
            else:
                outs[j][...] = total
        if into is not None:
            store = pltpu.make_async_copy(
                scr[0], outs[len(pieces)].at[pl.ds(into[1], stored)], scr[1]
            )
            store.start()
            store.wait()
        if fetch is not None:
            cut.wait()

    return chain(body, name, operands, in_specs, out_shape, out_specs, scratch, aliases)


def last_grad(chain, grad, far, w_self, far_cross):
    tokens, width = grad.shape
    steps = max(1, tokens // 512)

    def body(grad_ref, far_ref, a_ref, c_ref, out_ref):
        total = times_trans(grad_ref[...], a_ref[0]) + times_trans(far_ref[...], c_ref[0, 0])
        out_ref[...] = total.astype(jnp.bfloat16)

    rows = pl.BlockSpec((tokens // steps, width), lambda i: (i, 0))
    return chain(
        body,
        "last_grad",
        [grad, far, w_self, far_cross],
        [rows, rows, weight_block(w_self, 0), cross_block(far_cross)],
        [jax.ShapeDtypeStruct(grad.shape, grad.dtype)],
        [rows],
        grid=steps,
    )[0]


def cross_block(far_cross):
    return pl.BlockSpec((1, 1) + far_cross.shape[2:], lambda i: (other_core(), 0, 0, 0))


def other_core():
    return 1 - lax.axis_index("narrow") % 2


def both_cores(array):
    size = lax.axis_size("narrow")
    pairs = [[i, i + 1] for i in range(0, size, 2)]
    return lax.all_gather(array, "narrow", axis=0, axis_index_groups=pairs)


def weight_block(w_self, level):
    return pl.BlockSpec((1,) + w_self.shape[1:], lambda i: (level, 0, 0))


def weight_sums(chain, xs, sides, pairs, start, before, scale, last, name):
    rows = sum(g.shape[0] for g in sides[0])
    width = xs[0][0].shape[-1]
    parts = lax.axis_size("wide")
    share = width // parts
    n = len(pairs)
    operands = [x for x, _ in xs]
    in_specs = [ANY] * len(xs)
    for side in sides:
        operands += side if isinstance(side, list) else [in_hbm(side)]
        in_specs += [WHOLE] * len(side) if isinstance(side, list) else [ANY]
    if before is not None:
        operands.append(before)
        in_specs.append(WHOLE)
    buffers = [x for x, _ in xs] + [side for side in sides if not isinstance(side, list)]

    def body(*refs):
        ins, rest = list(refs[: len(operands)]), refs[len(operands) :]
        outs, scratch = rest[: len(out_shape)], rest[len(out_shape) :]
        old = None if before is None else ins.pop()
        total = scratch[-1] if last else outs[0]
        copies = []

        def fetch(source):
            j = len(copies)
            copy = pltpu.make_async_copy(source, scratch[0].at[j], scratch[1].at[j])
            copy.start()
            copies.append(copy)
            return scratch[0].at[j]

        x_bufs = [fetch(ins.pop(0).at[(*where(), pl.ds(start, rows))]) for _, where in xs]
        side_refs = []
        for side in sides:
            if isinstance(side, list):
                side_refs.append([ins.pop(0) for _ in side])
            else:
                side_refs.append([fetch(ins.pop(0).at[pl.ds(start, rows)])])
        for copy in copies:
            copy.wait()
        for j, (x, side) in enumerate(pairs):
            at = 0
            acc = None if before is None else old[j]
            for ref in side_refs[side]:
                size = ref.shape[0]
                term = outer_sum(x_bufs[x][at : at + size], ref[...])
                acc = term if acc is None else acc + term
                at += size
            total[j] = acc * scale if last else acc
        if last:
            me = lax.axis_index("wide")
            at = 0
            for b, many in enumerate(last):
                for k in range(parts):
                    there = pl.multiple_of((me ^ k) * share, share)
                    out = outs[b * parts + k]
                    out[...] = total[at : at + many, pl.ds(there, share)].astype(out.dtype)
                at += many

    whole = jax.ShapeDtypeStruct((n, width, width), jnp.float32)
    out_shape = [whole]
    if last:
        out_shape = [
            jax.ShapeDtypeStruct((many, share, width), jnp.bfloat16 if k else jnp.float32)
            for many in last
            for k in range(parts)
        ]
    scratch = [
        pltpu.VMEM((len(buffers), rows, width), buffers[0].dtype),
        pltpu.SemaphoreType.DMA((len(buffers),)),
    ]
    if last:
        scratch.append(pltpu.VMEM(whole.shape, jnp.float32))
    return chain(
        body, name, operands, in_specs, out_shape, [WHOLE] * len(out_shape), scratch
    )


def add_terms(chain, terms, name, dtypes, hold=None):
    m = len(terms)
    n = m + (hold is not None)

    def body(*refs):
        for j, dtype in enumerate(dtypes):
            total = refs[0][j].astype(jnp.float32)
            for ref in refs[1:m]:
                total = total + ref[j].astype(jnp.float32)
            refs[n + j][...] = total.astype(dtype)

    out_shape = [jax.ShapeDtypeStruct(terms[0].shape[1:], d) for d in dtypes]
    out_specs = [WHOLE] * len(dtypes)
    if hold is None:
        return chain(body, name, terms, [WHOLE] * m, out_shape, out_specs)
    return chain(
        body,
        name,
        [*terms, in_hbm(hold)],
        [WHOLE] * m + [ANY],
        [*out_shape, jax.ShapeDtypeStruct(hold.shape, hold.dtype)],
        [*out_specs, ANY],
        aliases={m: len(dtypes)},
    )


def store_levels(chain, levels, name):
    flat, spans = [], []
    for entry in levels:
        entry = entry if isinstance(entry, list) else [entry]
        spans.append((len(flat), len(entry)))
        flat += entry
    shape = flat[0].shape[-2:]

    def body(*refs):
        out = refs[len(flat)]
        for j, (first, many) in enumerate(spans):
            total = None
            for ref in refs[first : first + many]:
                value = ref[...].reshape(shape).astype(jnp.float32)
                total = value if total is None else total + value
            out[j] = total

    return chain(
        body,
        name,
        flat,
        [WHOLE] * len(flat),
        [jax.ShapeDtypeStruct((len(levels),) + shape, jnp.float32)],
        [WHOLE],
    )[0]


def local(saved_inputs, cotangent, w_self, w_cross):
    tokens, width = cotangent.shape
    parts = lax.axis_size("wide")
    share = w_cross.shape[1] // parts
    scale = 1.0 / math.sqrt(tokens * parts)
    cuts = row_cuts(tokens)
    n = len(cuts)
    z = n - 1
    end = cuts[z][0]
    far_inputs, far_cross = both_cores(saved_inputs), both_cores(w_cross)
    saved_inputs, cotangent, w_cross = in_hbm(saved_inputs), in_hbm(cotangent), in_hbm(w_cross)
    far_inputs, far_cross = in_hbm(far_inputs), in_hbm(far_cross)
    chain = Chain()
    near = [[None] * n for _ in range(LEVELS)]
    far = [[None] * n for _ in range(LEVELS)]

    def spread(terms):
        return [terms[0]] + [swap(t, "wide", k) for k, t in enumerate(terms[1:], 1)]

    def send(level, k):
        far[level][k] = [swap(a, "narrow", 1 << level) for a in near[level][k]]

    def flat(arrays):
        return [a for group in arrays for a in group]

    def at_level(level):
        return lambda: (level,)

    halves_of = min(2, parts)
    first, half_1 = cut_out(
        chain,
        [
            [(w_cross, my_share(2, parts), share), (cotangent, rows_at(0), cuts[0][1])],
            [(w_cross, my_share(1, halves_of), width // halves_of)],
        ],
        "first_rows",
    )
    first = swap(first, "narrow", 1 << 2)
    half_1 = swap(half_1, "narrow", 1 << 1)
    share_2, rows, *starts = cut_out(
        chain,
        [
            [(first, rows_at(0), share)],
            [(first, rows_at(share), cuts[0][1])],
            [(cotangent, rows_at(cuts[0][0]), cuts[0][1])],
            [(cotangent, rows_at(cuts[1][0]), cuts[1][1])],
        ],
        "parted",
        VMEM_LIMIT,
    )
    far[2][0], near[2][0], near[2][1] = [rows], [starts[0]], [starts[1]]
    send(2, 1)
    shares_2 = [(share_2, place_of(0, parts))]
    shares_2 += [(swap(share_2, "wide", k), place_of(k, parts)) for k in range(1, parts)]
    shares_1 = [(half_1, place_of(0, halves_of))]
    shares_1 += [(swap(half_1, "wide", k), place_of(k, halves_of)) for k in range(1, halves_of)]
    self_2 = weight_sums(
        chain,
        [(saved_inputs, at_level(2))],
        [[cotangent]],
        [(0, 0)],
        0,
        None,
        scale,
        (1,),
        "self_sums_2",
    )
    self_2 = spread(self_2)
    blocks = [None, None, *join_shares(chain, [shares_2], "join_2")]

    def job(level, k):
        return (level, near[level][k][0], far[level][k][0], blocks[level])

    grad = jax.ShapeDtypeStruct(cotangent.shape, cotangent.dtype)

    def level_1(k):
        jobs = [(1, a, b, blocks[1]) for a, b in zip(near[1][k], far[1][k])]
        return next_grads(chain, w_self, jobs, f"next_grads_1_{k}", (grad, cuts[k][0]))[0]

    def sums_a(ks, before, last=None):
        xs = [(saved_inputs, at_level(2)), (saved_inputs, at_level(1))]
        sides = [flat(far[2][k] for k in ks), flat(near[1][k] for k in ks)]
        start, name = cuts[ks[0]][0], f"sums_a_{ks[0]}"
        return weight_sums(chain, xs, sides, [(0, 0), (1, 1)], start, before, scale, last, name)

    def sums_b(k, before, last=None):
        xs = [(saved_inputs, at_level(1)), (saved_inputs, at_level(0))]
        xs.append((far_inputs, lambda: (other_core(), 0)))
        pairs = [(0, 0), (1, 1), (2, 1)]
        start, name = cuts[k][0], f"sums_b_{k}"
        return weight_sums(
            chain, xs, [far[1][k], grad], pairs, start, before, scale, last, name
        )

    sum_a = sum_b = None
    for k in range(n):
        ahead = k + 2
        done = next_grads(
            chain,
            w_self,
            [job(2, k)] + ([job(1, 0)] if k == 1 else []),
            f"next_grads_{k}",
            (grad, 0) if k == 1 else None,
            False,
            (cotangent, *cuts[ahead]) if ahead < n else None,
        )
        if ahead < n:
            near[2][ahead] = [done.pop()]
            send(2, ahead)
        if k == 1:
            grad = done.pop()
        near[1][k] = done
        send(1, k)
        if k == 0:
            (self_2,) = add_terms(chain, self_2, "add_self_2", (jnp.float32,))
            (blocks[1],) = join_shares(chain, [shares_1], "join_1")
        if 2 <= k < z:
            grad = level_1(k - 1) if k < z - 1 else grad
        if 1 <= k < z - 1:
            (sum_b,) = sums_b(k - 1, sum_b)
        if 1 <= k < z:
            (sum_a,) = sums_a([0, 1] if k == 1 else [k], sum_a)
    sum_a = spread(sums_a([z], sum_a, (2,)))
    for k in (z - 2, z - 1):
        grad = level_1(k)
        (sum_b,) = sums_b(k, sum_b)
    grad = level_1(z)
    sum_b = spread(sums_b(z, sum_b, (3,)))
    cross_2, self_1, grad = add_terms(chain, sum_a, "add_a", (jnp.bfloat16, jnp.float32), grad)
    cross_2 = swap(cross_2, "narrow", 1 << 2)
    far_grad = swap(grad, "narrow", 1 << 0)
    out = last_grad(chain, grad, far_grad, w_self, far_cross)
    cross_1, self_0, cross_0 = add_terms(
        chain, sum_b, "add_b", (jnp.bfloat16, jnp.float32, jnp.float32)
    )
    cross_1 = swap(cross_1, "narrow", 1 << 1)
    grad_self = store_levels(chain, [self_0, self_1, self_2], "store_self")
    grad_cross = store_levels(chain, [cross_0, cross_1, cross_2], "store_cross")
    return out, grad_self, grad_cross


def solution(mesh):
    in_specs = (
        P(None, "wide", "narrow"),
        P("wide", "narrow"),
        P(None, "narrow", None),
        P(None, "narrow", None),
    )
    out_specs = (
        P("wide", "narrow"),
        P(None, ("narrow", "wide"), None),
        P(None, ("narrow", "wide"), None),
    )
    return jax.shard_map(local, mesh=mesh, in_specs=in_specs, out_specs=out_specs, check_vma=False)
```

```python
import math

import jax
import jax.numpy as jnp
from jax import lax
from jax.experimental import pallas as pl
from jax.experimental.pallas import tpu as pltpu
from jax.sharding import PartitionSpec as P

LEVELS = 3
TOP = LEVELS - 1
CUTS = (3, 6, 6, 7, 6, 4)
ROW_TILE = 16
VMEM_LIMIT = 24 * 1024 * 1024
WHOLE_VMEM = 60 * 1024 * 1024

ANY = pl.BlockSpec(memory_space=pl.ANY)
WHOLE = pl.BlockSpec(memory_space=pltpu.VMEM)
TOKEN = jax.ShapeDtypeStruct((8, 128), jnp.float32)


def in_hbm(array):
    return pltpu.with_memory_space_constraint(array, pltpu.HBM)


def swap(array, axis, mask):
    return lax.ppermute(array, axis, [(i, i ^ mask) for i in range(lax.axis_size(axis))])


def swap_both(array, wide_mask, narrow_mask):
    wide, narrow = lax.axis_size("wide"), lax.axis_size("narrow")
    pairs = [
        (w * narrow + i, (w ^ wide_mask) * narrow + (i ^ narrow_mask))
        for w in range(wide)
        for i in range(narrow)
    ]
    return lax.ppermute(array, ("wide", "narrow"), pairs)


def outer_sum(left, right):
    return lax.dot_general(
        left, right, (((0,), (0,)), ((), ())), preferred_element_type=jnp.float32
    )


def times_trans(left, right):
    return lax.dot_general(
        left, right, (((1,), (1,)), ((), ())), preferred_element_type=jnp.float32
    )


class Chain:
    def __init__(self):
        self.token = None

    def __call__(self, body, name, operands, in_specs, out_shape, out_specs, scratch=(), aliases=None, limit=VMEM_LIMIT, grid=1):
        n_in, n_out = len(operands), len(out_shape)
        held = [] if self.token is None else [self.token]

        def whole(*refs):
            ins = refs[:n_in]
            rest = refs[n_in + len(held) :]
            body(*ins, *rest[:n_out], *rest[n_out + 1 :])

        *outs, self.token = pl.pallas_call(
            whole,
            grid=(grid,),
            out_shape=[*out_shape, TOKEN],
            in_specs=[*in_specs] + [ANY] * len(held),
            out_specs=[*out_specs, ANY],
            scratch_shapes=list(scratch),
            input_output_aliases=aliases or {},
            compiler_params=pltpu.CompilerParams(vmem_limit_bytes=limit),
            name=name,
        )(*operands, *held)
        return outs


def row_cuts(tokens):
    unit = tokens // sum(CUTS)
    assert unit * sum(CUTS) == tokens and unit % ROW_TILE == 0
    cuts, start = [], 0
    for c in CUTS:
        cuts.append((start, c * unit))
        start += c * unit
    return cuts


def cut_out(chain, blocks, name, limit=WHOLE_VMEM, deps=()):
    flat = [piece for block in blocks for piece in block]
    n = len(flat)

    def body(*refs):
        copies = []
        for b, block in enumerate(blocks):
            at = 0
            for _, where, size in block:
                j = len(copies)
                target = refs[n + len(deps) + b].at[pl.ds(at, size)]
                copy = pltpu.make_async_copy(where(refs[j], size), target, refs[-1].at[j])
                copy.start()
                copies.append(copy)
                at += size
        for copy in copies:
            copy.wait()

    return chain(
        body,
        name,
        [piece[0] for piece in flat] + [in_hbm(a) for a in deps],
        [ANY] * (n + len(deps)),
        [
            jax.ShapeDtypeStruct((sum(p[2] for p in block), block[0][0].shape[-1]), block[0][0].dtype)
            for block in blocks
        ],
        [WHOLE] * len(blocks),
        [pltpu.SemaphoreType.DMA((n,))],
        limit=limit,
    )


def rows_at(start):
    return lambda ref, size: ref.at[pl.ds(start, size)]


def block_of(level):
    return lambda ref, size: ref.at[level]


def my_share(level):
    def where(ref, size):
        first = pl.multiple_of(lax.axis_index("wide") * size, size)
        return ref.at[level, pl.ds(first, size)]

    return where


def place_of(mask):
    return lambda: lax.axis_index("wide") ^ mask


def join_shares(chain, blocks, name):
    flat = [piece for block in blocks for piece in block]

    def body(*refs):
        ins, outs = list(refs[: len(flat)]), refs[len(flat) :]
        for out, block in zip(outs, blocks):
            for share, place in block:
                size = share.shape[0]
                out[pl.ds(pl.multiple_of(place() * size, size), size)] = ins.pop(0)[...]

    return chain(
        body,
        name,
        [share for share, _ in flat],
        [WHOLE] * len(flat),
        [
            jax.ShapeDtypeStruct((sum(a.shape[0] for a, _ in block),) + block[0][0].shape[1:], block[0][0].dtype)
            for block in blocks
        ],
        [WHOLE] * len(blocks),
    )


def next_grads(chain, w_self, jobs, name, into=None, fetch=(), deps=(), block=None):
    width = w_self.shape[2]
    operands, in_specs, out_shape, out_specs, scratch, aliases = [], [], [], [], [], {}
    for level, grad, far, far_cross in jobs:
        operands += [w_self, far_cross, grad, far]
        in_specs += [weight_block(w_self, level), WHOLE, WHOLE, WHOLE]
    rows = [job[1].shape[0] for job in jobs]
    for size, job in zip(rows, jobs):
        if job[0] != 1:
            out_shape.append(jax.ShapeDtypeStruct((size, width), jnp.bfloat16))
            out_specs.append(WHOLE)
    n_kept = len(out_shape)
    for array, _, _, size in fetch:
        operands.append(array)
        in_specs.append(ANY)
        out_shape.append(jax.ShapeDtypeStruct((size, array.shape[-1]), array.dtype))
        out_specs.append(WHOLE)
    operands += deps
    in_specs += [ANY] * len(deps)
    n_moved = len(fetch) + (2 if block is not None else 0)
    if n_moved:
        scratch.append(pltpu.SemaphoreType.DMA((n_moved,)))
    if block is not None:
        operands.append(block[0])
        in_specs.append(ANY)
        scratch.append(pltpu.VMEM((width, width), jnp.bfloat16))
    if into is not None:
        if not isinstance(into[0], jax.ShapeDtypeStruct):
            aliases[len(operands)] = len(out_shape)
            operands.append(in_hbm(into[0]))
            in_specs.append(ANY)
        out_shape.append(jax.ShapeDtypeStruct(into[0].shape, into[0].dtype))
        out_specs.append(ANY)
        stored = sum(size for size, job in zip(rows, jobs) if job[0] == 1)
        scratch += [pltpu.VMEM((stored, width), jnp.bfloat16), pltpu.SemaphoreType.DMA]

    def body(*refs):
        ins, rest = refs[: len(operands)], refs[len(operands) :]
        outs, scr = rest[: len(out_shape)], rest[len(out_shape) :]
        first = 4 * len(jobs)
        copies = []
        for f, (_, index, start, size) in enumerate(fetch):
            source = ins[first + f].at[(*index, pl.ds(start, size))]
            copies.append(pltpu.make_async_copy(source, outs[n_kept + f], scr[0].at[f]))
        if block is not None:
            source = ins[first + len(fetch) + len(deps)].at[block[1]]
            copies.append(pltpu.make_async_copy(source, scr[1], scr[0].at[n_moved - 2]))
        for copy in copies:
            copy.start()
        at = 0
        for j in range(len(jobs)):
            a_ref, c_ref, grad_ref, far_ref = ins[4 * j : 4 * j + 4]
            total = times_trans(grad_ref[...], a_ref[0]) + times_trans(far_ref[...], c_ref[...])
            total = total.astype(jnp.bfloat16)
            if jobs[j][0] == 1:
                scr[-2][at : at + rows[j]] = total
                at += rows[j]
            else:
                outs[j][...] = total
        stores = []
        if into is not None:
            target = outs[-1].at[pl.ds(into[1], stored)]
            stores.append(pltpu.make_async_copy(scr[-2], target, scr[-1]))
            stores[-1].start()
        for copy in copies:
            copy.wait()
        if block is not None:
            target = outs[-1].at[pl.ds(block[2], width)]
            stores.append(pltpu.make_async_copy(scr[1], target, scr[0].at[n_moved - 1]))
            stores[-1].start()
        for copy in stores:
            copy.wait()

    return chain(body, name, operands, in_specs, out_shape, out_specs, scratch, aliases)


def last_grad(chain, both, far_both, w_self, tokens):
    width = both.shape[1]
    steps = max(1, tokens // width)

    def body(grad_ref, far_ref, a_ref, c_ref, out_ref):
        total = times_trans(grad_ref[...], a_ref[0]) + times_trans(far_ref[...], c_ref[...])
        out_ref[...] = total.astype(jnp.bfloat16)

    rows = pl.BlockSpec((tokens // steps, width), lambda i: (i, 0))
    return chain(
        body,
        "last_grad",
        [in_hbm(both), in_hbm(far_both), w_self, in_hbm(far_both)],
        [rows, rows, weight_block(w_self, 0), pl.BlockSpec((width, width), lambda i: (tokens // width, 0))],
        [jax.ShapeDtypeStruct((tokens, width), both.dtype)],
        [rows],
        grid=steps,
    )[0]


def weight_block(w_self, level):
    return pl.BlockSpec((1,) + w_self.shape[1:], lambda i: (level, 0, 0))


def weight_sums(chain, xs, sides, pairs, start, before, scale, last, name):
    rows = sum(g.shape[0] for g in sides[0])
    width = xs[0][0].shape[-1]
    parts = lax.axis_size("wide")
    share = width // parts
    n = len(pairs)
    operands = [x for x, _, _ in xs]
    in_specs = [ANY] * len(xs)
    for side in sides:
        operands += side if isinstance(side, list) else [in_hbm(side)]
        in_specs += [WHOLE] * len(side) if isinstance(side, list) else [ANY]
    if before is not None:
        operands.append(before)
        in_specs.append(WHOLE)
    buffers = [x for x, _, _ in xs] + [side for side in sides if not isinstance(side, list)]

    def body(*refs):
        ins, rest = list(refs[: len(operands)]), refs[len(operands) :]
        outs, scratch = rest[: len(out_shape)], rest[len(out_shape) :]
        old = None if before is None else ins.pop()
        total = scratch[-1] if last else outs[0]
        copies = []

        def fetch(source):
            j = len(copies)
            copy = pltpu.make_async_copy(source, scratch[0].at[j], scratch[1].at[j])
            copy.start()
            copies.append(copy)
            return scratch[0].at[j]

        x_bufs = [fetch(ins.pop(0).at[(*at, pl.ds(start - zero, rows))]) for _, at, zero in xs]
        side_refs = []
        for side in sides:
            if isinstance(side, list):
                side_refs.append([ins.pop(0) for _ in side])
            else:
                side_refs.append([fetch(ins.pop(0).at[pl.ds(start, rows)])])
        for copy in copies:
            copy.wait()
        for j, (x, side) in enumerate(pairs):
            at = 0
            acc = None if before is None else old[j]
            for ref in side_refs[side]:
                size = ref.shape[0]
                term = outer_sum(x_bufs[x][at : at + size], ref[...])
                acc = term if acc is None else acc + term
                at += size
            total[j] = acc * scale if last else acc
        if last:
            me = lax.axis_index("wide")
            at = 0
            for b, many in enumerate(abs(size) for size in last):
                for k in range(parts):
                    there = pl.multiple_of((me ^ k) * share, share)
                    out = outs[b * parts + k]
                    out[...] = total[at : at + many, pl.ds(there, share)].astype(out.dtype)
                at += many

    whole = jax.ShapeDtypeStruct((n, width, width), jnp.float32)
    out_shape = [whole]
    if last:
        out_shape = [
            jax.ShapeDtypeStruct(
                (abs(many), share, width), jnp.bfloat16 if k or many < 0 else jnp.float32
            )
            for many in last
            for k in range(parts)
        ]
    scratch = [
        pltpu.VMEM((len(buffers), rows, width), buffers[0].dtype),
        pltpu.SemaphoreType.DMA((len(buffers),)),
    ]
    if last:
        scratch.append(pltpu.VMEM(whole.shape, jnp.float32))
    return chain(
        body, name, operands, in_specs, out_shape, [WHOLE] * len(out_shape), scratch
    )


def add_terms(chain, terms, name, dtypes, hold=None):
    m = len(terms)
    n = m + (hold is not None)

    def body(*refs):
        for j, dtype in enumerate(dtypes):
            total = refs[0][j].astype(jnp.float32)
            for ref in refs[1:m]:
                total = total + ref[j].astype(jnp.float32)
            refs[n + j][...] = total.astype(dtype)

    out_shape = [jax.ShapeDtypeStruct(terms[0].shape[1:], d) for d in dtypes]
    out_specs = [WHOLE] * len(dtypes)
    if hold is None:
        return chain(body, name, terms, [WHOLE] * m, out_shape, out_specs)
    return chain(
        body,
        name,
        [*terms, in_hbm(hold)],
        [WHOLE] * m + [ANY],
        [*out_shape, jax.ShapeDtypeStruct(hold.shape, hold.dtype)],
        [*out_specs, ANY],
        aliases={m: len(dtypes)},
    )


def last_sums(chain, cross_1, terms, self_1, self_2, cross_2):
    m, n = len(cross_1), len(terms)
    shape = terms[0].shape[1:]

    def added(refs, j):
        value = refs[0][j].astype(jnp.float32)
        for ref in refs[1:]:
            value = value + ref[j].astype(jnp.float32)
        return value

    def body(*refs):
        one, two = refs[:m], refs[m : m + n]
        self_1_ref, self_2_ref, cross_2_ref, self_ref, cross_ref = refs[m + n :]
        self_ref[0] = added(two, 0)
        self_ref[1] = self_1_ref[...]
        self_ref[2] = self_2_ref[...]
        cross_ref[0] = added(two, 1)
        cross_ref[1] = added(one, 0)
        cross_ref[2] = cross_2_ref[...].astype(jnp.float32)

    levels = jax.ShapeDtypeStruct((LEVELS,) + shape, jnp.float32)
    return chain(
        body,
        "last_sums",
        [*cross_1, *terms, self_1, self_2, cross_2],
        [WHOLE] * (m + n + 3),
        [levels, levels],
        [WHOLE, WHOLE],
    )


def local(saved_inputs, cotangent, w_self, w_cross):
    tokens, width = cotangent.shape
    parts = lax.axis_size("wide")
    share = w_cross.shape[1] // parts
    scale = 1.0 / math.sqrt(tokens * parts)
    cuts = row_cuts(tokens)
    n = len(cuts)
    z = n - 1
    end = cuts[z][0]
    far_inputs = swap(saved_inputs, "narrow", 1 << 0)
    saved_inputs, cotangent, w_cross = in_hbm(saved_inputs), in_hbm(cotangent), in_hbm(w_cross)
    chain = Chain()
    near = [[None] * n for _ in range(LEVELS)]
    far = [[None] * n for _ in range(LEVELS)]

    def spread(terms):
        return [terms[0]] + [swap(t, "wide", k) for k, t in enumerate(terms[1:], 1)]

    def send(level, k):
        far[level][k] = [swap(a, "narrow", 1 << level) for a in near[level][k]]

    def flat(arrays):
        return [a for group in arrays for a in group]

    first, cross_1 = cut_out(
        chain,
        [
            [(w_cross, my_share(2), share), (cotangent, rows_at(0), cuts[0][1])],
            [(w_cross, block_of(1), width)],
        ],
        "first_rows",
        VMEM_LIMIT,
    )
    cross_1 = swap(cross_1, "narrow", 1 << 1)
    first = swap(first, "narrow", 1 << 2)
    self_2 = weight_sums(
        chain,
        [(saved_inputs, (2,), 0)],
        [[cotangent]],
        [(0, 0)],
        0,
        None,
        scale,
        (1,),
        "self_sums_2",
    )
    self_2 = spread(self_2)
    (self_2,) = add_terms(chain, self_2, "add_self_2", (jnp.float32,))
    share_2, rows, *starts = cut_out(
        chain,
        [
            [(first, rows_at(0), share)],
            [(first, rows_at(share), cuts[0][1])],
            [(cotangent, rows_at(cuts[0][0]), cuts[0][1])],
            [(cotangent, rows_at(cuts[1][0]), cuts[1][1])],
        ],
        "parted",
        VMEM_LIMIT,
        [far_inputs],
    )
    far_inputs = in_hbm(far_inputs)
    far[2][0], near[2][0], near[2][1] = [rows], [starts[0]], [starts[1]]
    send(2, 1)
    shares_2 = [(share_2, place_of(0))]
    shares_2 += [(swap(share_2, "wide", k), place_of(k)) for k in range(1, parts)]
    blocks = [None, cross_1, *join_shares(chain, [shares_2], "join_2")]

    def job(level, k):
        return (level, near[level][k][0], far[level][k][0], blocks[level])

    grad = jax.ShapeDtypeStruct((tokens + width, width), cotangent.dtype)

    def level_1(ks, block=None):
        jobs = [job(1, k) for k in ks]
        into = (grad, cuts[ks[0]][0])
        return next_grads(chain, w_self, jobs, f"next_grads_1_{ks[0]}", into, (), (), block)

    def sums_a(ks, before, last=None):
        xs = [(saved_inputs, (2,), 0), (saved_inputs, (1,), 0)]
        sides = [flat(far[2][k] for k in ks), flat(near[1][k] for k in ks)]
        start, name = cuts[ks[0]][0], f"sums_a_{ks[0]}"
        return weight_sums(chain, xs, sides, [(0, 0), (1, 1)], start, before, scale, last, name)

    def sums_b(ks, before, last=None):
        xs = [(saved_inputs, (1,), 0), (saved_inputs, (0,), 0), (far_inputs, (0,), 0)]
        pairs = [(0, 0), (1, 1), (2, 1)]
        start, name = cuts[ks[0]][0], f"sums_b_{ks[0]}"
        side = flat(far[1][k] for k in ks)
        return weight_sums(chain, xs, [side, grad], pairs, start, before, scale, last, name)

    sum_a = sum_b = None
    for k in range(n):
        ahead = k + 2
        done = next_grads(
            chain,
            w_self,
            [job(2, k)] + ([job(1, 0)] if k == 1 else []),
            f"next_grads_{k}",
            (grad, 0) if k == 1 else None,
            [(cotangent, (), *cuts[ahead])] if ahead < n else [],
        )
        if k == 1:
            grad = done.pop()
        if ahead < n:
            near[2][ahead] = [done.pop()]
            send(2, ahead)
        near[1][k] = done
        send(1, k)
        if 2 <= k < z - 1:
            block = (w_cross, 0, tokens) if k == 2 else None
            (grad,) = level_1([k - 1], block)
        if 1 <= k < z - 1:
            (sum_b,) = sums_b([k - 1], sum_b)
        if 1 <= k < z:
            (sum_a,) = sums_a([0, 1] if k == 1 else [k], sum_a)
    sum_a = spread(sums_a([z], sum_a, (2,)))
    for k in (z - 2, z - 1):
        (grad,) = level_1([k])
        (sum_b,) = sums_b([k], sum_b)
    (grad,) = level_1([z])
    terms = sums_b([z], sum_b, (-1, 2))
    cross_1 = [swap_both(t, k, 1 << 1) for k, t in enumerate(terms[:parts])]
    sum_c = spread(terms[parts:])
    cross_2, self_1, grad = add_terms(chain, sum_a, "add_a", (jnp.bfloat16, jnp.float32), grad)
    cross_2 = swap(cross_2, "narrow", 1 << 2)
    far_grad = swap(grad, "narrow", 1 << 0)
    out = last_grad(chain, grad, far_grad, w_self, tokens)
    grad_self, grad_cross = last_sums(chain, cross_1, sum_c, self_1, self_2, cross_2)
    return out, grad_self, grad_cross


def solution(mesh):
    in_specs = (
        P(None, "wide", "narrow"),
        P("wide", "narrow"),
        P(None, "narrow", None),
        P(None, "narrow", None),
    )
    out_specs = (
        P("wide", "narrow"),
        P(None, ("narrow", "wide"), None),
        P(None, ("narrow", "wide"), None),
    )
    return jax.shard_map(local, mesh=mesh, in_specs=in_specs, out_specs=out_specs, check_vma=False)
```

```python
import math

import jax
import jax.numpy as jnp
from jax import lax
from jax.experimental import pallas as pl
from jax.experimental.pallas import tpu as pltpu
from jax.sharding import PartitionSpec as P

LEVELS = 3
TOP = LEVELS - 1
CUTS = (3, 6, 6, 7, 6, 4)
ROW_TILE = 16
VMEM_LIMIT = 24 * 1024 * 1024
WHOLE_VMEM = 60 * 1024 * 1024

ANY = pl.BlockSpec(memory_space=pl.ANY)
WHOLE = pl.BlockSpec(memory_space=pltpu.VMEM)
TOKEN = jax.ShapeDtypeStruct((8, 128), jnp.float32)


def in_hbm(array):
    return pltpu.with_memory_space_constraint(array, pltpu.HBM)


def swap(array, axis, mask):
    return lax.ppermute(array, axis, [(i, i ^ mask) for i in range(lax.axis_size(axis))])


def swap_both(array, wide_mask, narrow_mask):
    wide, narrow = lax.axis_size("wide"), lax.axis_size("narrow")
    pairs = [
        (w * narrow + i, (w ^ wide_mask) * narrow + (i ^ narrow_mask))
        for w in range(wide)
        for i in range(narrow)
    ]
    return lax.ppermute(array, ("wide", "narrow"), pairs)


def outer_sum(left, right):
    return lax.dot_general(
        left, right, (((0,), (0,)), ((), ())), preferred_element_type=jnp.float32
    )


def times_trans(left, right):
    return lax.dot_general(
        left, right, (((1,), (1,)), ((), ())), preferred_element_type=jnp.float32
    )


class Chain:
    def __init__(self):
        self.token = None

    def __call__(self, body, name, operands, in_specs, out_shape, out_specs, scratch=(), aliases=None, limit=VMEM_LIMIT, grid=1):
        n_in, n_out = len(operands), len(out_shape)
        held = [] if self.token is None else [self.token]

        def whole(*refs):
            ins = refs[:n_in]
            rest = refs[n_in + len(held) :]
            body(*ins, *rest[:n_out], *rest[n_out + 1 :])

        *outs, self.token = pl.pallas_call(
            whole,
            grid=(grid,),
            out_shape=[*out_shape, TOKEN],
            in_specs=[*in_specs] + [ANY] * len(held),
            out_specs=[*out_specs, ANY],
            scratch_shapes=list(scratch),
            input_output_aliases=aliases or {},
            compiler_params=pltpu.CompilerParams(vmem_limit_bytes=limit),
            name=name,
        )(*operands, *held)
        return outs


def row_cuts(tokens):
    unit = tokens // sum(CUTS)
    assert unit * sum(CUTS) == tokens and unit % ROW_TILE == 0
    cuts, start = [], 0
    for c in CUTS:
        cuts.append((start, c * unit))
        start += c * unit
    return cuts


def cut_out(chain, blocks, name, limit=WHOLE_VMEM, deps=()):
    flat = [piece for block in blocks for piece in block]
    n = len(flat)

    def body(*refs):
        copies = []
        for b, block in enumerate(blocks):
            at = 0
            for _, where, size in block:
                j = len(copies)
                target = refs[n + len(deps) + b].at[pl.ds(at, size)]
                copy = pltpu.make_async_copy(where(refs[j], size), target, refs[-1].at[j])
                copy.start()
                copies.append(copy)
                at += size
        for copy in copies:
            copy.wait()

    return chain(
        body,
        name,
        [piece[0] for piece in flat] + list(deps),
        [ANY] * (n + len(deps)),
        [
            jax.ShapeDtypeStruct((sum(p[2] for p in block), block[0][0].shape[-1]), block[0][0].dtype)
            for block in blocks
        ],
        [WHOLE] * len(blocks),
        [pltpu.SemaphoreType.DMA((n,))],
        limit=limit,
    )


def rows_at(start):
    return lambda ref, size: ref.at[pl.ds(start, size)]


def block_of(level):
    return lambda ref, size: ref.at[level]


def my_share(level):
    def where(ref, size):
        first = pl.multiple_of(lax.axis_index("wide") * size, size)
        return ref.at[level, pl.ds(first, size)]

    return where


def place_of(mask):
    return lambda: lax.axis_index("wide") ^ mask


def join_shares(chain, blocks, name):
    flat = [piece for block in blocks for piece in block]

    def body(*refs):
        ins, outs = list(refs[: len(flat)]), refs[len(flat) :]
        for out, block in zip(outs, blocks):
            for share, place in block:
                size = share.shape[0]
                out[pl.ds(pl.multiple_of(place() * size, size), size)] = ins.pop(0)[...]

    return chain(
        body,
        name,
        [share for share, _ in flat],
        [WHOLE] * len(flat),
        [
            jax.ShapeDtypeStruct((sum(a.shape[0] for a, _ in block),) + block[0][0].shape[1:], block[0][0].dtype)
            for block in blocks
        ],
        [WHOLE] * len(blocks),
    )


def next_grads(chain, w_self, jobs, name, into=None, fetch=(), deps=(), block=None):
    width = w_self.shape[2]
    operands, in_specs, out_shape, out_specs, scratch, aliases = [], [], [], [], [], {}
    for level, grad, far, far_cross in jobs:
        operands += [w_self, far_cross, grad, far]
        in_specs += [weight_block(w_self, level), WHOLE, WHOLE, WHOLE]
    rows = [job[1].shape[0] for job in jobs]
    for size, job in zip(rows, jobs):
        if job[0] != 1:
            out_shape.append(jax.ShapeDtypeStruct((size, width), jnp.bfloat16))
            out_specs.append(WHOLE)
    n_kept = len(out_shape)
    for array, _, _, size in fetch:
        operands.append(array)
        in_specs.append(ANY)
        out_shape.append(jax.ShapeDtypeStruct((size, array.shape[-1]), array.dtype))
        out_specs.append(WHOLE)
    operands += deps
    in_specs += [ANY] * len(deps)
    n_moved = len(fetch) + (2 if block is not None else 0)
    if n_moved:
        scratch.append(pltpu.SemaphoreType.DMA((n_moved,)))
    if block is not None:
        operands.append(block[0])
        in_specs.append(ANY)
        scratch.append(pltpu.VMEM((width, width), jnp.bfloat16))
    if into is not None:
        if not isinstance(into[0], jax.ShapeDtypeStruct):
            aliases[len(operands)] = len(out_shape)
            operands.append(into[0])
            in_specs.append(ANY)
        out_shape.append(jax.ShapeDtypeStruct(into[0].shape, into[0].dtype))
        out_specs.append(ANY)
        stored = sum(size for size, job in zip(rows, jobs) if job[0] == 1)
        scratch += [pltpu.VMEM((stored, width), jnp.bfloat16), pltpu.SemaphoreType.DMA]

    def body(*refs):
        ins, rest = refs[: len(operands)], refs[len(operands) :]
        outs, scr = rest[: len(out_shape)], rest[len(out_shape) :]
        first = 4 * len(jobs)
        copies = []
        for f, (_, index, start, size) in enumerate(fetch):
            source = ins[first + f].at[(*index, pl.ds(start, size))]
            copies.append(pltpu.make_async_copy(source, outs[n_kept + f], scr[0].at[f]))
        if block is not None:
            source = ins[first + len(fetch) + len(deps)].at[block[1]]
            copies.append(pltpu.make_async_copy(source, scr[1], scr[0].at[n_moved - 2]))
        for copy in copies:
            copy.start()
        at = 0
        for j in range(len(jobs)):
            a_ref, c_ref, grad_ref, far_ref = ins[4 * j : 4 * j + 4]
            total = times_trans(grad_ref[...], a_ref[0]) + times_trans(far_ref[...], c_ref[...])
            total = total.astype(jnp.bfloat16)
            if jobs[j][0] == 1:
                scr[-2][at : at + rows[j]] = total
                at += rows[j]
            else:
                outs[j][...] = total
        stores = []
        if into is not None:
            target = outs[-1].at[pl.ds(into[1], stored)]
            stores.append(pltpu.make_async_copy(scr[-2], target, scr[-1]))
            stores[-1].start()
        for copy in copies:
            copy.wait()
        if block is not None:
            target = outs[-1].at[pl.ds(block[2], width)]
            stores.append(pltpu.make_async_copy(scr[1], target, scr[0].at[n_moved - 1]))
            stores[-1].start()
        for copy in stores:
            copy.wait()

    return chain(body, name, operands, in_specs, out_shape, out_specs, scratch, aliases)


def last_grad(chain, both, far_both, w_self, tokens, hold):
    width = both.shape[1]
    steps = max(1, tokens // width)

    def body(grad_ref, far_ref, a_ref, c_ref, _, out_ref, __):
        total = times_trans(grad_ref[...], a_ref[0]) + times_trans(far_ref[...], c_ref[...])
        out_ref[...] = total.astype(jnp.bfloat16)

    rows = pl.BlockSpec((tokens // steps, width), lambda i: (i, 0))
    return chain(
        body,
        "last_grad",
        [both, far_both, w_self, far_both, hold],
        [rows, rows, weight_block(w_self, 0), pl.BlockSpec((width, width), lambda i: (tokens // width, 0)), ANY],
        [jax.ShapeDtypeStruct((tokens, width), both.dtype), jax.ShapeDtypeStruct(hold.shape, hold.dtype)],
        [rows, ANY],
        aliases={4: 1},
        grid=steps,
    )


def weight_block(w_self, level):
    return pl.BlockSpec((1,) + w_self.shape[1:], lambda i: (level, 0, 0))


def weight_sums(chain, xs, sides, pairs, start, before, scale, last, name):
    rows = sum(g.shape[0] for g in sides[0])
    width = xs[0][0].shape[-1]
    parts = lax.axis_size("wide")
    share = width // parts
    n = len(pairs)
    operands = [x for x, _, _ in xs]
    in_specs = [ANY] * len(xs)
    for side in sides:
        operands += side if isinstance(side, list) else [side]
        in_specs += [WHOLE] * len(side) if isinstance(side, list) else [ANY]
    if before is not None:
        operands.append(before)
        in_specs.append(WHOLE)
    buffers = [x for x, _, _ in xs] + [side for side in sides if not isinstance(side, list)]

    def body(*refs):
        ins, rest = list(refs[: len(operands)]), refs[len(operands) :]
        outs, scratch = rest[: len(out_shape)], rest[len(out_shape) :]
        old = None if before is None else ins.pop()
        total = scratch[-1] if last else outs[0]
        copies = []

        def fetch(source):
            j = len(copies)
            copy = pltpu.make_async_copy(source, scratch[0].at[j], scratch[1].at[j])
            copy.start()
            copies.append(copy)
            return scratch[0].at[j]

        x_bufs = [fetch(ins.pop(0).at[(*at, pl.ds(start - zero, rows))]) for _, at, zero in xs]
        side_refs = []
        for side in sides:
            if isinstance(side, list):
                side_refs.append([ins.pop(0) for _ in side])
            else:
                side_refs.append([fetch(ins.pop(0).at[pl.ds(start, rows)])])
        for copy in copies:
            copy.wait()
        for j, (x, side) in enumerate(pairs):
            at = 0
            acc = None if before is None else old[j]
            for ref in side_refs[side]:
                size = ref.shape[0]
                term = outer_sum(x_bufs[x][at : at + size], ref[...])
                acc = term if acc is None else acc + term
                at += size
            total[j] = acc * scale if last else acc
        if last:
            me = lax.axis_index("wide")
            at = 0
            for b, many in enumerate(abs(size) for size in last):
                for k in range(parts):
                    there = pl.multiple_of((me ^ k) * share, share)
                    out = outs[b * parts + k]
                    out[...] = total[at : at + many, pl.ds(there, share)].astype(out.dtype)
                at += many

    whole = jax.ShapeDtypeStruct((n, width, width), jnp.float32)
    out_shape = [whole]
    if last:
        out_shape = [
            jax.ShapeDtypeStruct(
                (abs(many), share, width), jnp.bfloat16 if k or many < 0 else jnp.float32
            )
            for many in last
            for k in range(parts)
        ]
    scratch = [
        pltpu.VMEM((len(buffers), rows, width), buffers[0].dtype),
        pltpu.SemaphoreType.DMA((len(buffers),)),
    ]
    if last:
        scratch.append(pltpu.VMEM(whole.shape, jnp.float32))
    return chain(
        body, name, operands, in_specs, out_shape, [WHOLE] * len(out_shape), scratch
    )


def add_terms(chain, terms, name, dtypes, hold=None):
    m = len(terms)
    n = m + (hold is not None)

    def body(*refs):
        for j, dtype in enumerate(dtypes):
            total = refs[0][j].astype(jnp.float32)
            for ref in refs[1:m]:
                total = total + ref[j].astype(jnp.float32)
            refs[n + j][...] = total.astype(dtype)

    out_shape = [jax.ShapeDtypeStruct(terms[0].shape[1:], d) for d in dtypes]
    out_specs = [WHOLE] * len(dtypes)
    if hold is None:
        return chain(body, name, terms, [WHOLE] * m, out_shape, out_specs)
    return chain(
        body,
        name,
        [*terms, hold],
        [WHOLE] * m + [ANY],
        [*out_shape, jax.ShapeDtypeStruct(hold.shape, hold.dtype)],
        [*out_specs, ANY],
        aliases={m: len(dtypes)},
    )


def last_sums(chain, cross_1, terms, self_1, self_2, cross_2):
    m, n = len(cross_1), len(terms)
    shape = terms[0].shape[1:]

    def added(refs, j):
        value = refs[0][j].astype(jnp.float32)
        for ref in refs[1:]:
            value = value + ref[j].astype(jnp.float32)
        return value

    def body(*refs):
        one, two = refs[:m], refs[m : m + n]
        self_1_ref, self_2_ref, cross_2_ref, self_ref, cross_ref = refs[m + n :]
        self_ref[0] = added(two, 0)
        self_ref[1] = self_1_ref[...]
        self_ref[2] = self_2_ref[...]
        cross_ref[0] = added(two, 1)
        cross_ref[1] = added(one, 0)
        cross_ref[2] = cross_2_ref[...].astype(jnp.float32)

    levels = jax.ShapeDtypeStruct((LEVELS,) + shape, jnp.float32)
    return chain(
        body,
        "last_sums",
        [*cross_1, *terms, self_1, self_2, cross_2],
        [WHOLE] * (m + n + 3),
        [levels, levels],
        [WHOLE, WHOLE],
    )


def local(saved_inputs, cotangent, w_self, w_cross):
    tokens, width = cotangent.shape
    parts = lax.axis_size("wide")
    share = w_cross.shape[1] // parts
    scale = 1.0 / math.sqrt(tokens * parts)
    cuts = row_cuts(tokens)
    n = len(cuts)
    z = n - 1
    end = cuts[z][0]
    far_inputs = swap(saved_inputs, "narrow", 1 << 0)
    saved_inputs, cotangent, w_cross = in_hbm(saved_inputs), in_hbm(cotangent), in_hbm(w_cross)
    chain = Chain()
    near = [[None] * n for _ in range(LEVELS)]
    far = [[None] * n for _ in range(LEVELS)]

    def spread(terms):
        return [terms[0]] + [swap(t, "wide", k) for k, t in enumerate(terms[1:], 1)]

    def send(level, k):
        far[level][k] = [swap(a, "narrow", 1 << level) for a in near[level][k]]

    def flat(arrays):
        return [a for group in arrays for a in group]

    first, cross_1 = cut_out(
        chain,
        [
            [(w_cross, my_share(2), share), (cotangent, rows_at(0), cuts[0][1])],
            [(w_cross, block_of(1), width)],
        ],
        "first_rows",
        VMEM_LIMIT,
    )
    cross_1 = swap(cross_1, "narrow", 1 << 1)
    first = swap(first, "narrow", 1 << 2)
    self_2 = weight_sums(
        chain,
        [(saved_inputs, (2,), 0)],
        [[cotangent]],
        [(0, 0)],
        0,
        None,
        scale,
        (1,),
        "self_sums_2",
    )
    self_2 = spread(self_2)
    (self_2,) = add_terms(chain, self_2, "add_self_2", (jnp.float32,))
    share_2, rows, *starts = cut_out(
        chain,
        [
            [(first, rows_at(0), share)],
            [(first, rows_at(share), cuts[0][1])],
            [(cotangent, rows_at(cuts[0][0]), cuts[0][1])],
            [(cotangent, rows_at(cuts[1][0]), cuts[1][1])],
        ],
        "parted",
        VMEM_LIMIT,
        [far_inputs],
    )
    far[2][0], near[2][0], near[2][1] = [rows], [starts[0]], [starts[1]]
    send(2, 1)
    shares_2 = [(share_2, place_of(0))]
    shares_2 += [(swap(share_2, "wide", k), place_of(k)) for k in range(1, parts)]
    blocks = [None, cross_1, *join_shares(chain, [shares_2], "join_2")]

    def job(level, k):
        return (level, near[level][k][0], far[level][k][0], blocks[level])

    grad = jax.ShapeDtypeStruct((tokens + width, width), cotangent.dtype)

    def level_1(ks, block=None, fetch=()):
        jobs = [job(1, k) for k in ks]
        into = (grad, cuts[ks[0]][0])
        return next_grads(chain, w_self, jobs, f"next_grads_1_{ks[0]}", into, fetch, (), block)

    def sums_a(ks, before, last=None):
        xs = [(saved_inputs, (2,), 0), (saved_inputs, (1,), 0)]
        sides = [flat(far[2][k] for k in ks), flat(near[1][k] for k in ks)]
        start, name = cuts[ks[0]][0], f"sums_a_{ks[0]}"
        return weight_sums(chain, xs, sides, [(0, 0), (1, 1)], start, before, scale, last, name)

    def sums_b(ks, before, last=None):
        xs = [(saved_inputs, (1,), 0), (saved_inputs, (0,), 0), (far_inputs, (0,), 0)]
        pairs = [(0, 0), (1, 1), (2, 1)]
        start, name = cuts[ks[0]][0], f"sums_b_{ks[0]}"
        side = flat(far[1][k] for k in ks)
        return weight_sums(chain, xs, [side, grad], pairs, start, before, scale, last, name)

    sum_a = sum_b = None
    for k in range(n):
        ahead = k + 2
        done = next_grads(
            chain,
            w_self,
            [job(2, k)] + ([job(1, 0)] if k == 1 else []),
            f"next_grads_{k}",
            (grad, 0) if k == 1 else None,
            [(cotangent, (), *cuts[ahead])] if ahead < min(4, n) else [],
        )
        if k == 1:
            grad = done.pop()
        if ahead < min(4, n):
            near[2][ahead] = [done.pop()]
            send(2, ahead)
        near[1][k] = done
        send(1, k)
        if 2 <= k < z - 1:
            block = (w_cross, 0, tokens) if k == 2 else None
            rows, grad = level_1([k - 1], block, [(cotangent, (), *cuts[ahead])])
            near[2][ahead] = [rows]
            send(2, ahead)
        if 1 <= k < z - 1:
            (sum_b,) = sums_b([k - 1], sum_b)
        if 1 <= k < z:
            (sum_a,) = sums_a([0, 1] if k == 1 else [k], sum_a)
    sum_a = spread(sums_a([z], sum_a, (2,)))
    for k in (z - 2, z - 1):
        (grad,) = level_1([k])
        (sum_b,) = sums_b([k], sum_b)
    (grad,) = level_1([z])
    terms = sums_b([z], sum_b, (-1, 2))
    cross_1 = [swap_both(t, k, 1 << 1) for k, t in enumerate(terms[:parts])]
    sum_c = spread(terms[parts:])
    cross_2, self_1, grad = add_terms(chain, sum_a, "add_a", (jnp.bfloat16, jnp.float32), grad)
    far_grad = swap(grad, "narrow", 1 << 0)
    out, cross_2 = last_grad(chain, grad, far_grad, w_self, tokens, cross_2)
    cross_2 = swap(cross_2, "narrow", 1 << 2)
    grad_self, grad_cross = last_sums(chain, cross_1, sum_c, self_1, self_2, cross_2)
    return out, grad_self, grad_cross


def solution(mesh):
    in_specs = (
        P(None, "wide", "narrow"),
        P("wide", "narrow"),
        P(None, "narrow", None),
        P(None, "narrow", None),
    )
    out_specs = (
        P("wide", "narrow"),
        P(None, ("narrow", "wide"), None),
        P(None, ("narrow", "wide"), None),
    )
    return jax.shard_map(local, mesh=mesh, in_specs=in_specs, out_specs=out_specs, check_vma=False)
```

```python
import math

import jax
import jax.numpy as jnp
from jax import lax
from jax.experimental import pallas as pl
from jax.experimental.pallas import tpu as pltpu
from jax.sharding import PartitionSpec as P

LEVELS = 3
TOP = LEVELS - 1
CUTS = (3, 6, 6, 7, 6, 4)
ROW_TILE = 16
VMEM_LIMIT = 24 * 1024 * 1024

ANY = pl.BlockSpec(memory_space=pl.ANY)
WHOLE = pl.BlockSpec(memory_space=pltpu.VMEM)
TOKEN = jax.ShapeDtypeStruct((8, 128), jnp.float32)


def in_hbm(array):
    return pltpu.with_memory_space_constraint(array, pltpu.HBM)


def swap(array, axis, mask):
    return lax.ppermute(array, axis, [(i, i ^ mask) for i in range(lax.axis_size(axis))])


def swap_both(array, wide_mask, narrow_mask):
    wide, narrow = lax.axis_size("wide"), lax.axis_size("narrow")
    pairs = [
        (w * narrow + i, (w ^ wide_mask) * narrow + (i ^ narrow_mask))
        for w in range(wide)
        for i in range(narrow)
    ]
    return lax.ppermute(array, ("wide", "narrow"), pairs)


def outer_sum(left, right):
    return lax.dot_general(
        left, right, (((0,), (0,)), ((), ())), preferred_element_type=jnp.float32
    )


def times_trans(left, right):
    return lax.dot_general(
        left, right, (((1,), (1,)), ((), ())), preferred_element_type=jnp.float32
    )


class Chain:
    def __init__(self):
        self.token = None

    def __call__(self, body, name, operands, in_specs, out_shape, out_specs, scratch=(), aliases=None, grid=1):
        n_in, n_out = len(operands), len(out_shape)
        held = [] if self.token is None else [self.token]

        def whole(*refs):
            ins = refs[:n_in]
            rest = refs[n_in + len(held) :]
            body(*ins, *rest[:n_out], *rest[n_out + 1 :])

        *outs, self.token = pl.pallas_call(
            whole,
            grid=(grid,),
            out_shape=[*out_shape, TOKEN],
            in_specs=[*in_specs] + [ANY] * len(held),
            out_specs=[*out_specs, ANY],
            scratch_shapes=list(scratch),
            input_output_aliases=aliases or {},
            compiler_params=pltpu.CompilerParams(vmem_limit_bytes=VMEM_LIMIT),
            name=name,
        )(*operands, *held)
        return outs


def row_cuts(tokens):
    unit = tokens // sum(CUTS)
    assert unit * sum(CUTS) == tokens and unit % ROW_TILE == 0
    cuts, start = [], 0
    for c in CUTS:
        cuts.append((start, c * unit))
        start += c * unit
    return cuts


def cut_out(chain, blocks, name, deps=()):
    flat = [piece for block in blocks for piece in block]
    n = len(flat)

    def body(*refs):
        copies = []
        for b, block in enumerate(blocks):
            at = 0
            for _, where, size in block:
                j = len(copies)
                target = refs[n + len(deps) + b].at[pl.ds(at, size)]
                copy = pltpu.make_async_copy(where(refs[j], size), target, refs[-1].at[j])
                copy.start()
                copies.append(copy)
                at += size
        for copy in copies:
            copy.wait()

    return chain(
        body,
        name,
        [piece[0] for piece in flat] + list(deps),
        [ANY] * (n + len(deps)),
        [
            jax.ShapeDtypeStruct((sum(p[2] for p in block), block[0][0].shape[-1]), block[0][0].dtype)
            for block in blocks
        ],
        [WHOLE] * len(blocks),
        [pltpu.SemaphoreType.DMA((n,))],
    )


def rows_at(start):
    return lambda ref, size: ref.at[pl.ds(start, size)]


def block_of(level):
    return lambda ref, size: ref.at[level]


def my_share(level):
    def where(ref, size):
        first = pl.multiple_of(lax.axis_index("wide") * size, size)
        return ref.at[level, pl.ds(first, size)]

    return where


def place_of(mask):
    return lambda: lax.axis_index("wide") ^ mask


def join_shares(chain, blocks, name):
    flat = [piece for block in blocks for piece in block]

    def body(*refs):
        ins, outs = list(refs[: len(flat)]), refs[len(flat) :]
        for out, block in zip(outs, blocks):
            for share, place in block:
                size = share.shape[0]
                out[pl.ds(pl.multiple_of(place() * size, size), size)] = ins.pop(0)[...]

    return chain(
        body,
        name,
        [share for share, _ in flat],
        [WHOLE] * len(flat),
        [
            jax.ShapeDtypeStruct((sum(a.shape[0] for a, _ in block),) + block[0][0].shape[1:], block[0][0].dtype)
            for block in blocks
        ],
        [WHOLE] * len(blocks),
    )


def next_grads(chain, w_self, jobs, name, into=None, block=None):
    width = w_self.shape[2]
    operands, in_specs, out_shape, out_specs, scratch, aliases = [], [], [], [], [], {}
    for level, grad, far, far_cross in jobs:
        operands += [w_self, far_cross, grad, far]
        in_specs += [weight_block(w_self, level), WHOLE, WHOLE, WHOLE]
    rows = [job[1].shape[0] for job in jobs]
    for size, job in zip(rows, jobs):
        if job[0] != 1:
            out_shape.append(jax.ShapeDtypeStruct((size, width), jnp.bfloat16))
            out_specs.append(WHOLE)
    if block is not None:
        operands.append(block[0])
        in_specs.append(ANY)
        scratch += [pltpu.SemaphoreType.DMA((2,)), pltpu.VMEM((width, width), jnp.bfloat16)]
    if into is not None:
        if not isinstance(into[0], jax.ShapeDtypeStruct):
            aliases[len(operands)] = len(out_shape)
            operands.append(into[0])
            in_specs.append(ANY)
        out_shape.append(jax.ShapeDtypeStruct(into[0].shape, into[0].dtype))
        out_specs.append(ANY)
        stored = sum(size for size, job in zip(rows, jobs) if job[0] == 1)
        scratch += [pltpu.VMEM((stored, width), jnp.bfloat16), pltpu.SemaphoreType.DMA]

    def body(*refs):
        ins, rest = refs[: len(operands)], refs[len(operands) :]
        outs, scr = rest[: len(out_shape)], rest[len(out_shape) :]
        if block is not None:
            move = pltpu.make_async_copy(ins[4 * len(jobs)].at[block[1]], scr[1], scr[0].at[0])
            move.start()
        at = 0
        for j in range(len(jobs)):
            a_ref, c_ref, grad_ref, far_ref = ins[4 * j : 4 * j + 4]
            total = times_trans(grad_ref[...], a_ref[0]) + times_trans(far_ref[...], c_ref[...])
            total = total.astype(jnp.bfloat16)
            if jobs[j][0] == 1:
                scr[-2][at : at + rows[j]] = total
                at += rows[j]
            else:
                outs[j][...] = total
        stores = []
        if into is not None:
            target = outs[-1].at[pl.ds(into[1], stored)]
            stores.append(pltpu.make_async_copy(scr[-2], target, scr[-1]))
            stores[-1].start()
        if block is not None:
            move.wait()
            target = outs[-1].at[pl.ds(block[2], width)]
            stores.append(pltpu.make_async_copy(scr[1], target, scr[0].at[1]))
            stores[-1].start()
        for copy in stores:
            copy.wait()

    return chain(body, name, operands, in_specs, out_shape, out_specs, scratch, aliases)


def last_grad(chain, both, far_both, w_self, tokens):
    width = both.shape[1]
    steps = max(1, tokens // width)

    def body(grad_ref, far_ref, a_ref, c_ref, out_ref):
        total = times_trans(grad_ref[...], a_ref[0]) + times_trans(far_ref[...], c_ref[...])
        out_ref[...] = total.astype(jnp.bfloat16)

    rows = pl.BlockSpec((tokens // steps, width), lambda i: (i, 0))
    return chain(
        body,
        "last_grad",
        [both, far_both, w_self, far_both],
        [rows, rows, weight_block(w_self, 0), pl.BlockSpec((width, width), lambda i: (tokens // width, 0))],
        [jax.ShapeDtypeStruct((tokens, width), both.dtype)],
        [rows],
        grid=steps,
    )[0]


def weight_block(w_self, level):
    return pl.BlockSpec((1,) + w_self.shape[1:], lambda i: (level, 0, 0))


def weight_sums(chain, xs, sides, pairs, start, before, scale, last, name):
    rows = sum(g.shape[0] for g in sides[0])
    width = xs[0][0].shape[-1]
    parts = lax.axis_size("wide")
    share = width // parts
    n = len(pairs)
    operands = [x for x, _, _ in xs]
    in_specs = [ANY] * len(xs)
    for side in sides:
        operands += side if isinstance(side, list) else [side]
        in_specs += [WHOLE] * len(side) if isinstance(side, list) else [ANY]
    if before is not None:
        operands.append(before)
        in_specs.append(WHOLE)
    buffers = [x for x, _, _ in xs] + [side for side in sides if not isinstance(side, list)]

    def body(*refs):
        ins, rest = list(refs[: len(operands)]), refs[len(operands) :]
        outs, scratch = rest[: len(out_shape)], rest[len(out_shape) :]
        old = None if before is None else ins.pop()
        total = scratch[-1] if last else outs[0]
        copies = []

        def fetch(source):
            j = len(copies)
            copy = pltpu.make_async_copy(source, scratch[0].at[j], scratch[1].at[j])
            copy.start()
            copies.append(copy)
            return scratch[0].at[j]

        x_bufs = [fetch(ins.pop(0).at[(*at, pl.ds(start - zero, rows))]) for _, at, zero in xs]
        side_refs = []
        for side in sides:
            if isinstance(side, list):
                side_refs.append([ins.pop(0) for _ in side])
            else:
                side_refs.append([fetch(ins.pop(0).at[pl.ds(start, rows)])])
        for copy in copies:
            copy.wait()
        for j, (x, side) in enumerate(pairs):
            at = 0
            acc = None if before is None else old[j]
            for ref in side_refs[side]:
                size = ref.shape[0]
                term = outer_sum(x_bufs[x][at : at + size], ref[...])
                acc = term if acc is None else acc + term
                at += size
            total[j] = acc * scale if last else acc
        if last:
            me = lax.axis_index("wide")
            at = 0
            for b, many in enumerate(abs(size) for size in last):
                for k in range(parts):
                    there = pl.multiple_of((me ^ k) * share, share)
                    out = outs[b * parts + k]
                    out[...] = total[at : at + many, pl.ds(there, share)].astype(out.dtype)
                at += many

    whole = jax.ShapeDtypeStruct((n, width, width), jnp.float32)
    out_shape = [whole]
    if last:
        out_shape = [
            jax.ShapeDtypeStruct(
                (abs(many), share, width), jnp.bfloat16 if k or many < 0 else jnp.float32
            )
            for many in last
            for k in range(parts)
        ]
    scratch = [
        pltpu.VMEM((len(buffers), rows, width), buffers[0].dtype),
        pltpu.SemaphoreType.DMA((len(buffers),)),
    ]
    if last:
        scratch.append(pltpu.VMEM(whole.shape, jnp.float32))
    return chain(
        body, name, operands, in_specs, out_shape, [WHOLE] * len(out_shape), scratch
    )


def add_terms(chain, terms, name, dtypes, hold=None):
    m = len(terms)
    n = m + (hold is not None)

    def body(*refs):
        for j, dtype in enumerate(dtypes):
            total = refs[0][j].astype(jnp.float32)
            for ref in refs[1:m]:
                total = total + ref[j].astype(jnp.float32)
            refs[n + j][...] = total.astype(dtype)

    out_shape = [jax.ShapeDtypeStruct(terms[0].shape[1:], d) for d in dtypes]
    out_specs = [WHOLE] * len(dtypes)
    if hold is None:
        return chain(body, name, terms, [WHOLE] * m, out_shape, out_specs)
    return chain(
        body,
        name,
        [*terms, hold],
        [WHOLE] * m + [ANY],
        [*out_shape, jax.ShapeDtypeStruct(hold.shape, hold.dtype)],
        [*out_specs, ANY],
        aliases={m: len(dtypes)},
    )


def hand_on(chain, arrays, deps, name):
    n = len(arrays)
    return chain(
        lambda *refs: None,
        name,
        [*arrays, *deps],
        [ANY] * (n + len(deps)),
        [jax.ShapeDtypeStruct(a.shape, a.dtype) for a in arrays],
        [ANY] * n,
        aliases={j: j for j in range(n)},
    )


def last_sums(chain, cross_1, terms, self_1, self_2, cross_2):
    m, n = len(cross_1), len(terms)
    shape = terms[0].shape[1:]

    def added(refs, j):
        value = refs[0][j].astype(jnp.float32)
        for ref in refs[1:]:
            value = value + ref[j].astype(jnp.float32)
        return value

    def body(*refs):
        one, two = refs[:m], refs[m : m + n]
        self_1_ref, self_2_ref, cross_2_ref, self_ref, cross_ref = refs[m + n :]
        self_ref[0] = added(two, 0)
        self_ref[1] = self_1_ref[...]
        self_ref[2] = self_2_ref[...]
        cross_ref[0] = added(two, 1)
        cross_ref[1] = added(one, 0)
        cross_ref[2] = cross_2_ref[...].astype(jnp.float32)

    levels = jax.ShapeDtypeStruct((LEVELS,) + shape, jnp.float32)
    return chain(
        body,
        "last_sums",
        [*cross_1, *terms, self_1, self_2, cross_2],
        [WHOLE] * (m + n + 3),
        [levels, levels],
        [WHOLE, WHOLE],
    )


def local(saved_inputs, cotangent, w_self, w_cross):
    tokens, width = cotangent.shape
    parts = lax.axis_size("wide")
    share = w_cross.shape[1] // parts
    scale = 1.0 / math.sqrt(tokens * parts)
    cuts = row_cuts(tokens)
    n = len(cuts)
    z = n - 1
    end = cuts[z][0]
    far_inputs = swap(saved_inputs, "narrow", 1 << 0)
    saved_inputs, cotangent, w_cross = in_hbm(saved_inputs), in_hbm(cotangent), in_hbm(w_cross)
    chain = Chain()
    near = [[None] * n for _ in range(LEVELS)]
    far = [[None] * n for _ in range(LEVELS)]

    def spread(terms):
        return [terms[0]] + [swap(t, "wide", k) for k, t in enumerate(terms[1:], 1)]

    def send(level, k):
        far[level][k] = [swap(a, "narrow", 1 << level) for a in near[level][k]]

    def flat(arrays):
        return [a for group in arrays for a in group]

    first, cross_1 = cut_out(
        chain,
        [
            [(w_cross, my_share(2), share), (cotangent, rows_at(0), cuts[0][1])],
            [(w_cross, block_of(1), width)],
        ],
        "first_rows",
    )
    cross_1 = swap(cross_1, "narrow", 1 << 1)
    first = swap(first, "narrow", 1 << 2)
    self_2 = weight_sums(
        chain,
        [(saved_inputs, (2,), 0)],
        [[cotangent]],
        [(0, 0)],
        0,
        None,
        scale,
        (1,),
        "self_sums_2",
    )
    self_2 = spread(self_2)
    (self_2,) = add_terms(chain, self_2, "add_self_2", (jnp.float32,))
    share_2, rows, *starts = cut_out(
        chain,
        [
            [(first, rows_at(0), share)],
            [(first, rows_at(share), cuts[0][1])],
            [(cotangent, rows_at(cuts[0][0]), cuts[0][1])],
            [(cotangent, rows_at(cuts[1][0]), cuts[1][1])],
        ],
        "parted",
        [far_inputs],
    )
    far[2][0], near[2][0], near[2][1] = [rows], [starts[0]], [starts[1]]
    send(2, 1)
    shares_2 = [(share_2, place_of(0))]
    shares_2 += [(swap(share_2, "wide", k), place_of(k)) for k in range(1, parts)]
    blocks = [None, cross_1, *join_shares(chain, [shares_2], "join_2")]

    def job(level, k):
        return (level, near[level][k][0], far[level][k][0], blocks[level])

    grad = jax.ShapeDtypeStruct((tokens + width, width), cotangent.dtype)

    def level_1(ks, block=None):
        jobs = [job(1, k) for k in ks]
        into = (grad, cuts[ks[0]][0])
        return next_grads(chain, w_self, jobs, f"next_grads_1_{ks[0]}", into, block)

    def sums_a(ks, before, last=None):
        xs = [(saved_inputs, (2,), 0), (saved_inputs, (1,), 0)]
        sides = [flat(far[2][k] for k in ks), flat(near[1][k] for k in ks)]
        start, name = cuts[ks[0]][0], f"sums_a_{ks[0]}"
        return weight_sums(chain, xs, sides, [(0, 0), (1, 1)], start, before, scale, last, name)

    def sums_b(ks, before, last=None):
        xs = [(saved_inputs, (1,), 0), (saved_inputs, (0,), 0), (far_inputs, (0,), 0)]
        pairs = [(0, 0), (1, 1), (2, 1)]
        start, name = cuts[ks[0]][0], f"sums_b_{ks[0]}"
        side = flat(far[1][k] for k in ks)
        return weight_sums(chain, xs, [side, grad], pairs, start, before, scale, last, name)

    def leave(k):
        rows = (cotangent, rows_at(cuts[k][0]), cuts[k][1])
        near[2][k] = cut_out(chain, [[rows]], f"rows_{k}")
        send(2, k)

    sum_a = sum_b = None
    for k in range(n):
        jobs = [job(2, k)] + ([job(1, 0)] if k == 1 else [])
        near[1][k] = next_grads(chain, w_self, jobs, f"next_grads_{k}", (grad, 0) if k == 1 else None)
        if k == 1:
            grad = near[1][k].pop()
        send(1, k)
        if k < 2:
            leave(k + 2)
        if 2 <= k < z - 1:
            (grad,) = level_1([k - 1], (w_cross, 0, tokens) if k == 2 else None)
            leave(k + 2)
        if 1 <= k < z - 1:
            (sum_b,) = sums_b([k - 1], sum_b)
        if 1 <= k < z:
            (sum_a,) = sums_a([0, 1] if k == 1 else [k], sum_a)
    sum_a = spread(sums_a([z], sum_a, (2,)))
    for k in (z - 2, z - 1):
        (grad,) = level_1([k])
        (sum_b,) = sums_b([k], sum_b)
    (grad,) = level_1([z])
    terms = sums_b([z], sum_b, (-1, 2))
    sum_c = spread(terms[parts:])
    cross_2, self_1, grad = add_terms(chain, sum_a, "add_a", (jnp.bfloat16, jnp.float32), grad)
    far_grad = swap(grad, "narrow", 1 << 0)
    cross_1 = [swap_both(terms[0], 0, 1 << 1)]
    cross_2, *terms = hand_on(chain, [cross_2, *terms[1:parts]], [far_grad], "rest")
    cross_1 += [swap_both(t, k, 1 << 1) for k, t in enumerate(terms, 1)]
    cross_2 = swap(cross_2, "narrow", 1 << 2)
    out = last_grad(chain, grad, far_grad, w_self, tokens)
    grad_self, grad_cross = last_sums(chain, cross_1, sum_c, self_1, self_2, cross_2)
    return out, grad_self, grad_cross


def solution(mesh):
    in_specs = (
        P(None, "wide", "narrow"),
        P("wide", "narrow"),
        P(None, "narrow", None),
        P(None, "narrow", None),
    )
    out_specs = (
        P("wide", "narrow"),
        P(None, ("narrow", "wide"), None),
        P(None, ("narrow", "wide"), None),
    )
    return jax.shard_map(local, mesh=mesh, in_specs=in_specs, out_specs=out_specs, check_vma=False)
```

```python
import math

import jax
import jax.numpy as jnp
from jax import lax
from jax.experimental import pallas as pl
from jax.experimental.pallas import tpu as pltpu
from jax.sharding import PartitionSpec as P

LEVELS = 3
TOP = LEVELS - 1
CUTS = (3, 6, 6, 7, 6, 4)
ROW_TILE = 16
VMEM_LIMIT = 24 * 1024 * 1024

ANY = pl.BlockSpec(memory_space=pl.ANY)
WHOLE = pl.BlockSpec(memory_space=pltpu.VMEM)
TOKEN = jax.ShapeDtypeStruct((8, 128), jnp.float32)


def in_hbm(array):
    return pltpu.with_memory_space_constraint(array, pltpu.HBM)


def swap(array, axis, mask):
    return lax.ppermute(array, axis, [(i, i ^ mask) for i in range(lax.axis_size(axis))])


def swap_both(array, wide_mask, narrow_mask):
    wide, narrow = lax.axis_size("wide"), lax.axis_size("narrow")
    pairs = [
        (w * narrow + i, (w ^ wide_mask) * narrow + (i ^ narrow_mask))
        for w in range(wide)
        for i in range(narrow)
    ]
    return lax.ppermute(array, ("wide", "narrow"), pairs)


def outer_sum(left, right):
    return lax.dot_general(
        left, right, (((0,), (0,)), ((), ())), preferred_element_type=jnp.float32
    )


def times_trans(left, right):
    return lax.dot_general(
        left, right, (((1,), (1,)), ((), ())), preferred_element_type=jnp.float32
    )


class Chain:
    def __init__(self):
        self.token = None

    def __call__(self, body, name, operands, in_specs, out_shape, out_specs, scratch=(), aliases=None, grid=1):
        n_in, n_out = len(operands), len(out_shape)
        held = [] if self.token is None else [self.token]

        def whole(*refs):
            ins = refs[:n_in]
            rest = refs[n_in + len(held) :]
            body(*ins, *rest[:n_out], *rest[n_out + 1 :])

        *outs, self.token = pl.pallas_call(
            whole,
            grid=(grid,),
            out_shape=[*out_shape, TOKEN],
            in_specs=[*in_specs] + [ANY] * len(held),
            out_specs=[*out_specs, ANY],
            scratch_shapes=list(scratch),
            input_output_aliases=aliases or {},
            compiler_params=pltpu.CompilerParams(vmem_limit_bytes=VMEM_LIMIT),
            name=name,
        )(*operands, *held)
        return outs


def row_cuts(tokens):
    unit = tokens // sum(CUTS)
    assert unit * sum(CUTS) == tokens and unit % ROW_TILE == 0
    cuts, start = [], 0
    for c in CUTS:
        cuts.append((start, c * unit))
        start += c * unit
    return cuts


def cut_out(chain, blocks, name, deps=()):
    flat = [piece for block in blocks for piece in block]
    n = len(flat)

    def body(*refs):
        copies = []
        for b, block in enumerate(blocks):
            at = 0
            for _, where, size in block:
                j = len(copies)
                target = refs[n + len(deps) + b].at[pl.ds(at, size)]
                copy = pltpu.make_async_copy(where(refs[j], size), target, refs[-1].at[j])
                copy.start()
                copies.append(copy)
                at += size
        for copy in copies:
            copy.wait()

    return chain(
        body,
        name,
        [piece[0] for piece in flat] + list(deps),
        [ANY] * (n + len(deps)),
        [
            jax.ShapeDtypeStruct((sum(p[2] for p in block), block[0][0].shape[-1]), block[0][0].dtype)
            for block in blocks
        ],
        [WHOLE] * len(blocks),
        [pltpu.SemaphoreType.DMA((n,))],
    )


def rows_at(start):
    return lambda ref, size: ref.at[pl.ds(start, size)]


def block_of(level):
    return lambda ref, size: ref.at[level]


def my_share(level):
    def where(ref, size):
        first = pl.multiple_of(lax.axis_index("wide") * size, size)
        return ref.at[level, pl.ds(first, size)]

    return where


def place_of(mask):
    return lambda: lax.axis_index("wide") ^ mask


def join_shares(chain, blocks, name):
    flat = [piece for block in blocks for piece in block]

    def body(*refs):
        ins, outs = list(refs[: len(flat)]), refs[len(flat) :]
        for out, block in zip(outs, blocks):
            for share, place in block:
                size = share.shape[0]
                out[pl.ds(pl.multiple_of(place() * size, size), size)] = ins.pop(0)[...]

    return chain(
        body,
        name,
        [share for share, _ in flat],
        [WHOLE] * len(flat),
        [
            jax.ShapeDtypeStruct((sum(a.shape[0] for a, _ in block),) + block[0][0].shape[1:], block[0][0].dtype)
            for block in blocks
        ],
        [WHOLE] * len(blocks),
    )


def next_grads(chain, w_self, jobs, name, into=None, block=None):
    width = w_self.shape[2]
    operands, in_specs, out_shape, out_specs, scratch, aliases = [], [], [], [], [], {}
    for level, grad, far, far_cross in jobs:
        operands += [w_self, far_cross, grad, far]
        in_specs += [weight_block(w_self, level), WHOLE, WHOLE, WHOLE]
    rows = [job[1].shape[0] for job in jobs]
    for size, job in zip(rows, jobs):
        if job[0] != 1:
            out_shape.append(jax.ShapeDtypeStruct((size, width), jnp.bfloat16))
            out_specs.append(WHOLE)
    if block is not None:
        operands.append(block[0])
        in_specs.append(ANY)
        scratch += [pltpu.SemaphoreType.DMA((2,)), pltpu.VMEM((width, width), jnp.bfloat16)]
    if into is not None:
        if not isinstance(into[0], jax.ShapeDtypeStruct):
            aliases[len(operands)] = len(out_shape)
            operands.append(into[0])
            in_specs.append(ANY)
        out_shape.append(jax.ShapeDtypeStruct(into[0].shape, into[0].dtype))
        out_specs.append(ANY)
        stored = sum(size for size, job in zip(rows, jobs) if job[0] == 1)
        scratch += [pltpu.VMEM((stored, width), jnp.bfloat16), pltpu.SemaphoreType.DMA]

    def body(*refs):
        ins, rest = refs[: len(operands)], refs[len(operands) :]
        outs, scr = rest[: len(out_shape)], rest[len(out_shape) :]
        if block is not None:
            move = pltpu.make_async_copy(ins[4 * len(jobs)].at[block[1]], scr[1], scr[0].at[0])
            move.start()
        at = 0
        for j in range(len(jobs)):
            a_ref, c_ref, grad_ref, far_ref = ins[4 * j : 4 * j + 4]
            total = times_trans(grad_ref[...], a_ref[0]) + times_trans(far_ref[...], c_ref[...])
            total = total.astype(jnp.bfloat16)
            if jobs[j][0] == 1:
                scr[-2][at : at + rows[j]] = total
                at += rows[j]
            else:
                outs[j][...] = total
        stores = []
        if into is not None:
            target = outs[-1].at[pl.ds(into[1], stored)]
            stores.append(pltpu.make_async_copy(scr[-2], target, scr[-1]))
            stores[-1].start()
        if block is not None:
            move.wait()
            target = outs[-1].at[pl.ds(block[2], width)]
            stores.append(pltpu.make_async_copy(scr[1], target, scr[0].at[1]))
            stores[-1].start()
        for copy in stores:
            copy.wait()

    return chain(body, name, operands, in_specs, out_shape, out_specs, scratch, aliases)


def last_grad(chain, both, far_both, w_self, tokens):
    width = both.shape[1]
    steps = max(1, tokens // width)

    def body(grad_ref, far_ref, a_ref, c_ref, out_ref):
        total = times_trans(grad_ref[...], a_ref[0]) + times_trans(far_ref[...], c_ref[...])
        out_ref[...] = total.astype(jnp.bfloat16)

    rows = pl.BlockSpec((tokens // steps, width), lambda i: (i, 0))
    return chain(
        body,
        "last_grad",
        [both, far_both, w_self, far_both],
        [rows, rows, weight_block(w_self, 0), pl.BlockSpec((width, width), lambda i: (tokens // width, 0))],
        [jax.ShapeDtypeStruct((tokens, width), both.dtype)],
        [rows],
        grid=steps,
    )[0]


def weight_block(w_self, level):
    return pl.BlockSpec((1,) + w_self.shape[1:], lambda i: (level, 0, 0))


def weight_sums(chain, xs, sides, pairs, start, before, scale, last, name):
    rows = sum(g.shape[0] for g in sides[0])
    width = xs[0][0].shape[-1]
    parts = lax.axis_size("wide")
    share = width // parts
    n = len(pairs)
    operands = [x for x, _, _ in xs]
    in_specs = [ANY] * len(xs)
    for side in sides:
        operands += side if isinstance(side, list) else [side]
        in_specs += [WHOLE] * len(side) if isinstance(side, list) else [ANY]
    if before is not None:
        operands.append(before)
        in_specs.append(WHOLE)
    buffers = [x for x, _, _ in xs] + [side for side in sides if not isinstance(side, list)]

    def body(*refs):
        ins, rest = list(refs[: len(operands)]), refs[len(operands) :]
        outs, scratch = rest[: len(out_shape)], rest[len(out_shape) :]
        old = None if before is None else ins.pop()
        total = scratch[-1] if last else outs[0]
        copies = []

        def fetch(source):
            j = len(copies)
            copy = pltpu.make_async_copy(source, scratch[0].at[j], scratch[1].at[j])
            copy.start()
            copies.append(copy)
            return scratch[0].at[j]

        x_bufs = [fetch(ins.pop(0).at[(*at, pl.ds(start - zero, rows))]) for _, at, zero in xs]
        side_refs = []
        for side in sides:
            if isinstance(side, list):
                side_refs.append([ins.pop(0) for _ in side])
            else:
                side_refs.append([fetch(ins.pop(0).at[pl.ds(start, rows)])])
        for copy in copies:
            copy.wait()
        for j, (x, side) in enumerate(pairs):
            at = 0
            acc = None if before is None else old[j]
            for ref in side_refs[side]:
                size = ref.shape[0]
                term = outer_sum(x_bufs[x][at : at + size], ref[...])
                acc = term if acc is None else acc + term
                at += size
            total[j] = acc * scale if last else acc
        if last:
            me = lax.axis_index("wide")
            at = 0
            for b, many in enumerate(abs(size) for size in last):
                for k in range(parts):
                    there = pl.multiple_of((me ^ k) * share, share)
                    out = outs[b * parts + k]
                    out[...] = total[at : at + many, pl.ds(there, share)].astype(out.dtype)
                at += many

    whole = jax.ShapeDtypeStruct((n, width, width), jnp.float32)
    out_shape = [whole]
    if last:
        out_shape = [
            jax.ShapeDtypeStruct(
                (abs(many), share, width), jnp.bfloat16 if k or many < 0 else jnp.float32
            )
            for many in last
            for k in range(parts)
        ]
    scratch = [
        pltpu.VMEM((len(buffers), rows, width), buffers[0].dtype),
        pltpu.SemaphoreType.DMA((len(buffers),)),
    ]
    if last:
        scratch.append(pltpu.VMEM(whole.shape, jnp.float32))
    return chain(
        body, name, operands, in_specs, out_shape, [WHOLE] * len(out_shape), scratch
    )


def add_terms(chain, terms, name, dtypes, hold=None):
    m = len(terms)
    n = m + (hold is not None)

    def body(*refs):
        for j, dtype in enumerate(dtypes):
            total = refs[0][j].astype(jnp.float32)
            for ref in refs[1:m]:
                total = total + ref[j].astype(jnp.float32)
            refs[n + j][...] = total.astype(dtype)

    out_shape = [jax.ShapeDtypeStruct(terms[0].shape[1:], d) for d in dtypes]
    out_specs = [WHOLE] * len(dtypes)
    if hold is None:
        return chain(body, name, terms, [WHOLE] * m, out_shape, out_specs)
    return chain(
        body,
        name,
        [*terms, hold],
        [WHOLE] * m + [ANY],
        [*out_shape, jax.ShapeDtypeStruct(hold.shape, hold.dtype)],
        [*out_specs, ANY],
        aliases={m: len(dtypes)},
    )


def hand_on(chain, arrays, deps, name):
    n = len(arrays)
    return chain(
        lambda *refs: None,
        name,
        [*arrays, *deps],
        [ANY] * (n + len(deps)),
        [jax.ShapeDtypeStruct(a.shape, a.dtype) for a in arrays],
        [ANY] * n,
        aliases={j: j for j in range(n)},
    )


def last_sums(chain, cross_1, terms, self_1, self_2, cross_2):
    m, n = len(cross_1), len(terms)
    shape = terms[0].shape[1:]

    def added(refs, j):
        value = refs[0][j].astype(jnp.float32)
        for ref in refs[1:]:
            value = value + ref[j].astype(jnp.float32)
        return value

    def body(*refs):
        cross_2_ref, one, two = refs[0], refs[1 : 1 + m], refs[1 + m : 1 + m + n]
        self_1_ref, self_2_ref, self_ref, cross_ref = refs[1 + m + n :]
        self_ref[0] = added(two, 0)
        self_ref[1] = self_1_ref[...]
        self_ref[2] = self_2_ref[...]
        cross_ref[0] = added(two, 1)
        cross_ref[1] = added(one, 0)
        cross_ref[2] = cross_2_ref[...].astype(jnp.float32)

    levels = jax.ShapeDtypeStruct((LEVELS,) + shape, jnp.float32)
    return chain(
        body,
        "last_sums",
        [cross_2, *cross_1, *terms, self_1, self_2],
        [WHOLE] * (m + n + 3),
        [levels, levels],
        [WHOLE, WHOLE],
    )


def local(saved_inputs, cotangent, w_self, w_cross):
    tokens, width = cotangent.shape
    parts = lax.axis_size("wide")
    share = w_cross.shape[1] // parts
    scale = 1.0 / math.sqrt(tokens * parts)
    cuts = row_cuts(tokens)
    n = len(cuts)
    z = n - 1
    end = cuts[z][0]
    far_inputs = swap(saved_inputs, "narrow", 1 << 0)
    saved_inputs, cotangent, w_cross = in_hbm(saved_inputs), in_hbm(cotangent), in_hbm(w_cross)
    chain = Chain()
    near = [[None] * n for _ in range(LEVELS)]
    far = [[None] * n for _ in range(LEVELS)]

    def spread(terms):
        return [terms[0]] + [swap(t, "wide", k) for k, t in enumerate(terms[1:], 1)]

    def send(level, k):
        far[level][k] = [swap(a, "narrow", 1 << level) for a in near[level][k]]

    def flat(arrays):
        return [a for group in arrays for a in group]

    first, cross_1 = cut_out(
        chain,
        [
            [(w_cross, my_share(2), share), (cotangent, rows_at(0), cuts[0][1])],
            [(w_cross, block_of(1), width)],
        ],
        "first_rows",
    )
    cross_1 = swap(cross_1, "narrow", 1 << 1)
    first = swap(first, "narrow", 1 << 2)
    self_2 = weight_sums(
        chain,
        [(saved_inputs, (2,), 0)],
        [[cotangent]],
        [(0, 0)],
        0,
        None,
        scale,
        (1,),
        "self_sums_2",
    )
    self_2 = spread(self_2)
    (self_2,) = add_terms(chain, self_2, "add_self_2", (jnp.float32,))
    share_2, rows, *starts = cut_out(
        chain,
        [
            [(first, rows_at(0), share)],
            [(first, rows_at(share), cuts[0][1])],
            [(cotangent, rows_at(cuts[0][0]), cuts[0][1])],
            [(cotangent, rows_at(cuts[1][0]), cuts[1][1])],
        ],
        "parted",
        [far_inputs],
    )
    far[2][0], near[2][0], near[2][1] = [rows], [starts[0]], [starts[1]]
    send(2, 1)
    shares_2 = [(share_2, place_of(0))]
    shares_2 += [(swap(share_2, "wide", k), place_of(k)) for k in range(1, parts)]
    blocks = [None, cross_1, *join_shares(chain, [shares_2], "join_2")]

    def job(level, k):
        return (level, near[level][k][0], far[level][k][0], blocks[level])

    grad = jax.ShapeDtypeStruct((tokens + width, width), cotangent.dtype)

    def level_1(ks, block=None):
        jobs = [job(1, k) for k in ks]
        into = (grad, cuts[ks[0]][0])
        return next_grads(chain, w_self, jobs, f"next_grads_1_{ks[0]}", into, block)

    def sums_a(ks, before, last=None):
        xs = [(saved_inputs, (2,), 0), (saved_inputs, (1,), 0)]
        sides = [flat(far[2][k] for k in ks), flat(near[1][k] for k in ks)]
        start, name = cuts[ks[0]][0], f"sums_a_{ks[0]}"
        return weight_sums(chain, xs, sides, [(0, 0), (1, 1)], start, before, scale, last, name)

    def sums_b(ks, before, last=None):
        xs = [(saved_inputs, (1,), 0), (saved_inputs, (0,), 0), (far_inputs, (0,), 0)]
        pairs = [(0, 0), (1, 1), (2, 1)]
        start, name = cuts[ks[0]][0], f"sums_b_{ks[0]}"
        side = flat(far[1][k] for k in ks)
        return weight_sums(chain, xs, [side, grad], pairs, start, before, scale, last, name)

    def leave(k):
        rows = (cotangent, rows_at(cuts[k][0]), cuts[k][1])
        near[2][k] = cut_out(chain, [[rows]], f"rows_{k}")
        send(2, k)

    sum_a = sum_b = None
    for k in range(n):
        jobs = [job(2, k)] + ([job(1, 0)] if k == 1 else [])
        near[1][k] = next_grads(chain, w_self, jobs, f"next_grads_{k}", (grad, 0) if k == 1 else None)
        if k == 1:
            grad = near[1][k].pop()
        send(1, k)
        if k < 2:
            leave(k + 2)
        if 2 <= k < z - 1:
            (grad,) = level_1([k - 1], (w_cross, 0, tokens) if k == 2 else None)
            leave(k + 2)
        if 1 <= k < z - 1:
            (sum_b,) = sums_b([k - 1], sum_b)
        if 1 <= k < z:
            (sum_a,) = sums_a([0, 1] if k == 1 else [k], sum_a)
    sum_a = spread(sums_a([z], sum_a, (2,)))
    for k in (z - 2, z - 1):
        (grad,) = level_1([k])
        (sum_b,) = sums_b([k], sum_b)
    (grad,) = level_1([z])
    terms = sums_b([z], sum_b, (-1, 2))
    sum_c = spread(terms[parts:])
    cross_2, self_1, grad = add_terms(chain, sum_a, "add_a", (jnp.bfloat16, jnp.float32), grad)
    far_grad = swap(grad, "narrow", 1 << 0)
    cross_1 = [swap_both(terms[0], 0, 1 << 1)]
    cross_2, *terms = hand_on(chain, [cross_2, *terms[1:parts]], [far_grad], "rest")
    cross_1 += [swap_both(t, k, 1 << 1) for k, t in enumerate(terms, 1)]
    cross_2 = swap(cross_2, "narrow", 1 << 2)
    out = last_grad(chain, grad, far_grad, w_self, tokens)
    grad_self, grad_cross = last_sums(chain, cross_1, sum_c, self_1, self_2, cross_2)
    return out, grad_self, grad_cross


def solution(mesh):
    in_specs = (
        P(None, "wide", "narrow"),
        P("wide", "narrow"),
        P(None, "narrow", None),
        P(None, "narrow", None),
    )
    out_specs = (
        P("wide", "narrow"),
        P(None, ("narrow", "wide"), None),
        P(None, ("narrow", "wide"), None),
    )
    return jax.shard_map(local, mesh=mesh, in_specs=in_specs, out_specs=out_specs, check_vma=False)
```

```python
import math

import jax
import jax.numpy as jnp
from jax import lax
from jax.experimental import pallas as pl
from jax.experimental.pallas import tpu as pltpu
from jax.sharding import PartitionSpec as P

LEVELS = 3
TOP = LEVELS - 1
CUTS = (3, 6, 6, 7, 6, 4)
ROW_TILE = 16
VMEM_LIMIT = 24 * 1024 * 1024

ANY = pl.BlockSpec(memory_space=pl.ANY)
WHOLE = pl.BlockSpec(memory_space=pltpu.VMEM)
TOKEN = jax.ShapeDtypeStruct((8, 128), jnp.float32)


def in_hbm(array):
    return pltpu.with_memory_space_constraint(array, pltpu.HBM)


def swap(array, axis, mask):
    return lax.ppermute(array, axis, [(i, i ^ mask) for i in range(lax.axis_size(axis))])


def swap_both(array, wide_mask, narrow_mask):
    wide, narrow = lax.axis_size("wide"), lax.axis_size("narrow")
    pairs = [
        (w * narrow + i, (w ^ wide_mask) * narrow + (i ^ narrow_mask))
        for w in range(wide)
        for i in range(narrow)
    ]
    return lax.ppermute(array, ("wide", "narrow"), pairs)


def outer_sum(left, right):
    return lax.dot_general(
        left, right, (((0,), (0,)), ((), ())), preferred_element_type=jnp.float32
    )


def times_trans(left, right):
    return lax.dot_general(
        left, right, (((1,), (1,)), ((), ())), preferred_element_type=jnp.float32
    )


class Chain:
    def __init__(self):
        self.token = None

    def __call__(self, body, name, operands, in_specs, out_shape, out_specs, scratch=(), aliases=None, grid=1):
        n_in, n_out = len(operands), len(out_shape)
        held = [] if self.token is None else [self.token]

        def whole(*refs):
            ins = refs[:n_in]
            rest = refs[n_in + len(held) :]
            body(*ins, *rest[:n_out], *rest[n_out + 1 :])

        *outs, self.token = pl.pallas_call(
            whole,
            grid=(grid,),
            out_shape=[*out_shape, TOKEN],
            in_specs=[*in_specs] + [ANY] * len(held),
            out_specs=[*out_specs, ANY],
            scratch_shapes=list(scratch),
            input_output_aliases=aliases or {},
            compiler_params=pltpu.CompilerParams(vmem_limit_bytes=VMEM_LIMIT),
            name=name,
        )(*operands, *held)
        return outs


def row_cuts(tokens):
    unit = tokens // sum(CUTS)
    assert unit * sum(CUTS) == tokens and unit % ROW_TILE == 0
    cuts, start = [], 0
    for c in CUTS:
        cuts.append((start, c * unit))
        start += c * unit
    return cuts


def cut_out(chain, blocks, name, deps=()):
    flat = [piece for block in blocks for piece in block]
    n = len(flat)

    def body(*refs):
        copies = []
        for b, block in enumerate(blocks):
            at = 0
            for _, where, size in block:
                j = len(copies)
                target = refs[n + len(deps) + b].at[pl.ds(at, size)]
                copy = pltpu.make_async_copy(where(refs[j], size), target, refs[-1].at[j])
                copy.start()
                copies.append(copy)
                at += size
        for copy in copies:
            copy.wait()

    return chain(
        body,
        name,
        [piece[0] for piece in flat] + list(deps),
        [ANY] * (n + len(deps)),
        [
            jax.ShapeDtypeStruct((sum(p[2] for p in block), block[0][0].shape[-1]), block[0][0].dtype)
            for block in blocks
        ],
        [WHOLE] * len(blocks),
        [pltpu.SemaphoreType.DMA((n,))],
    )


def rows_at(start):
    return lambda ref, size: ref.at[pl.ds(start, size)]


def block_of(level):
    return lambda ref, size: ref.at[level]


def my_share(level):
    def where(ref, size):
        first = pl.multiple_of(lax.axis_index("wide") * size, size)
        return ref.at[level, pl.ds(first, size)]

    return where


def place_of(mask):
    return lambda: lax.axis_index("wide") ^ mask


def join_shares(chain, blocks, name):
    flat = [piece for block in blocks for piece in block]

    def body(*refs):
        ins, outs = list(refs[: len(flat)]), refs[len(flat) :]
        for out, block in zip(outs, blocks):
            for share, place in block:
                size = share.shape[0]
                out[pl.ds(pl.multiple_of(place() * size, size), size)] = ins.pop(0)[...]

    return chain(
        body,
        name,
        [share for share, _ in flat],
        [WHOLE] * len(flat),
        [
            jax.ShapeDtypeStruct((sum(a.shape[0] for a, _ in block),) + block[0][0].shape[1:], block[0][0].dtype)
            for block in blocks
        ],
        [WHOLE] * len(blocks),
    )


def next_grads(chain, w_self, jobs, name, into=None, block=None):
    width = w_self.shape[2]
    operands, in_specs, out_shape, out_specs, scratch, aliases = [], [], [], [], [], {}
    for level, grad, far, far_cross in jobs:
        operands += [w_self, far_cross, grad, far]
        in_specs += [weight_block(w_self, level), WHOLE, WHOLE, WHOLE]
    rows = [job[1].shape[0] for job in jobs]
    for size, job in zip(rows, jobs):
        if job[0] != 1:
            out_shape.append(jax.ShapeDtypeStruct((size, width), jnp.bfloat16))
            out_specs.append(WHOLE)
    if block is not None:
        operands.append(block[0])
        in_specs.append(ANY)
        scratch += [pltpu.SemaphoreType.DMA((2,)), pltpu.VMEM((width, width), jnp.bfloat16)]
    if into is not None:
        if not isinstance(into[0], jax.ShapeDtypeStruct):
            aliases[len(operands)] = len(out_shape)
            operands.append(into[0])
            in_specs.append(ANY)
        out_shape.append(jax.ShapeDtypeStruct(into[0].shape, into[0].dtype))
        out_specs.append(ANY)
        stored = sum(size for size, job in zip(rows, jobs) if job[0] == 1)
        scratch += [pltpu.VMEM((stored, width), jnp.bfloat16), pltpu.SemaphoreType.DMA]

    def body(*refs):
        ins, rest = refs[: len(operands)], refs[len(operands) :]
        outs, scr = rest[: len(out_shape)], rest[len(out_shape) :]
        if block is not None:
            move = pltpu.make_async_copy(ins[4 * len(jobs)].at[block[1]], scr[1], scr[0].at[0])
            move.start()
        at = 0
        for j in range(len(jobs)):
            a_ref, c_ref, grad_ref, far_ref = ins[4 * j : 4 * j + 4]
            total = times_trans(grad_ref[...], a_ref[0]) + times_trans(far_ref[...], c_ref[...])
            total = total.astype(jnp.bfloat16)
            if jobs[j][0] == 1:
                scr[-2][at : at + rows[j]] = total
                at += rows[j]
            else:
                outs[j][...] = total
        stores = []
        if into is not None:
            target = outs[-1].at[pl.ds(into[1], stored)]
            stores.append(pltpu.make_async_copy(scr[-2], target, scr[-1]))
            stores[-1].start()
        if block is not None:
            move.wait()
            target = outs[-1].at[pl.ds(block[2], width)]
            stores.append(pltpu.make_async_copy(scr[1], target, scr[0].at[1]))
            stores[-1].start()
        for copy in stores:
            copy.wait()

    return chain(body, name, operands, in_specs, out_shape, out_specs, scratch, aliases)


def last_grad(chain, both, far_both, w_self, tokens):
    width = both.shape[1]
    steps = max(1, tokens // width)

    def body(grad_ref, far_ref, a_ref, c_ref, out_ref):
        total = times_trans(grad_ref[...], a_ref[0]) + times_trans(far_ref[...], c_ref[...])
        out_ref[...] = total.astype(jnp.bfloat16)

    rows = pl.BlockSpec((tokens // steps, width), lambda i: (i, 0))
    return chain(
        body,
        "last_grad",
        [both, far_both, w_self, far_both],
        [rows, rows, weight_block(w_self, 0), pl.BlockSpec((width, width), lambda i: (tokens // width, 0))],
        [jax.ShapeDtypeStruct((tokens, width), both.dtype)],
        [rows],
        grid=steps,
    )[0]


def weight_block(w_self, level):
    return pl.BlockSpec((1,) + w_self.shape[1:], lambda i: (level, 0, 0))


def weight_sums(chain, xs, sides, pairs, start, before, scale, last, name):
    rows = sum(g.shape[0] for g in sides[0])
    width = xs[0][0].shape[-1]
    parts = lax.axis_size("wide")
    share = width // parts
    n = len(pairs)
    operands = [x for x, _, _ in xs]
    in_specs = [ANY] * len(xs)
    for side in sides:
        operands += side if isinstance(side, list) else [side]
        in_specs += [WHOLE] * len(side) if isinstance(side, list) else [ANY]
    if before is not None:
        operands.append(before)
        in_specs.append(WHOLE)
    buffers = [x for x, _, _ in xs] + [side for side in sides if not isinstance(side, list)]

    def body(*refs):
        ins, rest = list(refs[: len(operands)]), refs[len(operands) :]
        outs, scratch = rest[: len(out_shape)], rest[len(out_shape) :]
        old = None if before is None else ins.pop()
        total = scratch[-1] if last else outs[0]
        copies = []

        def fetch(source):
            j = len(copies)
            copy = pltpu.make_async_copy(source, scratch[0].at[j], scratch[1].at[j])
            copy.start()
            copies.append(copy)
            return scratch[0].at[j]

        x_bufs = [fetch(ins.pop(0).at[(*at, pl.ds(start - zero, rows))]) for _, at, zero in xs]
        side_refs = []
        for side in sides:
            if isinstance(side, list):
                side_refs.append([ins.pop(0) for _ in side])
            else:
                side_refs.append([fetch(ins.pop(0).at[pl.ds(start, rows)])])
        for copy in copies:
            copy.wait()
        for j, (x, side) in enumerate(pairs):
            at = 0
            acc = None if before is None else old[j]
            for ref in side_refs[side]:
                size = ref.shape[0]
                term = outer_sum(x_bufs[x][at : at + size], ref[...])
                acc = term if acc is None else acc + term
                at += size
            total[j] = acc * scale if last else acc
        if last:
            me = lax.axis_index("wide")
            at = 0
            for b, many in enumerate(abs(size) for size in last):
                for k in range(parts):
                    there = pl.multiple_of((me ^ k) * share, share)
                    out = outs[b * parts + k]
                    out[...] = total[at : at + many, pl.ds(there, share)].astype(out.dtype)
                at += many

    whole = jax.ShapeDtypeStruct((n, width, width), jnp.float32)
    out_shape = [whole]
    if last:
        out_shape = [
            jax.ShapeDtypeStruct(
                (abs(many), share, width), jnp.bfloat16 if k or many < 0 else jnp.float32
            )
            for many in last
            for k in range(parts)
        ]
    scratch = [
        pltpu.VMEM((len(buffers), rows, width), buffers[0].dtype),
        pltpu.SemaphoreType.DMA((len(buffers),)),
    ]
    if last:
        scratch.append(pltpu.VMEM(whole.shape, jnp.float32))
    return chain(
        body, name, operands, in_specs, out_shape, [WHOLE] * len(out_shape), scratch
    )


def add_terms(chain, terms, name, dtypes, hold=None):
    m = len(terms)
    n = m + (hold is not None)

    def body(*refs):
        for j, dtype in enumerate(dtypes):
            total = refs[0][j].astype(jnp.float32)
            for ref in refs[1:m]:
                total = total + ref[j].astype(jnp.float32)
            refs[n + j][...] = total.astype(dtype)

    out_shape = [jax.ShapeDtypeStruct(terms[0].shape[1:], d) for d in dtypes]
    out_specs = [WHOLE] * len(dtypes)
    if hold is None:
        return chain(body, name, terms, [WHOLE] * m, out_shape, out_specs)
    return chain(
        body,
        name,
        [*terms, hold],
        [WHOLE] * m + [ANY],
        [*out_shape, jax.ShapeDtypeStruct(hold.shape, hold.dtype)],
        [*out_specs, ANY],
        aliases={m: len(dtypes)},
    )


def hand_on(chain, arrays, deps, name):
    n = len(arrays)
    return chain(
        lambda *refs: None,
        name,
        [*arrays, *deps],
        [ANY] * (n + len(deps)),
        [jax.ShapeDtypeStruct(a.shape, a.dtype) for a in arrays],
        [ANY] * n,
        aliases={j: j for j in range(n)},
    )


def last_sums(chain, cross_1, terms, self_1, self_2, cross_2):
    m, n = len(cross_1), len(terms)
    shape = terms[0].shape[1:]

    def added(refs, j):
        value = refs[0][j].astype(jnp.float32)
        for ref in refs[1:]:
            value = value + ref[j].astype(jnp.float32)
        return value

    def body(*refs):
        cross_2_ref, one, two = refs[0], refs[1 : 1 + m], refs[1 + m : 1 + m + n]
        self_1_ref, self_2_ref, self_ref, cross_ref = refs[1 + m + n :]
        self_ref[0] = added(two, 0)
        self_ref[1] = self_1_ref[...]
        self_ref[2] = self_2_ref[...]
        cross_ref[0] = added(two, 1)
        cross_ref[1] = added(one, 0)
        cross_ref[2] = cross_2_ref[...].astype(jnp.float32)

    levels = jax.ShapeDtypeStruct((LEVELS,) + shape, jnp.float32)
    return chain(
        body,
        "last_sums",
        [cross_2, *cross_1, *terms, self_1, self_2],
        [WHOLE] * (m + n + 3),
        [levels, levels],
        [WHOLE, WHOLE],
    )


def local(saved_inputs, cotangent, w_self, w_cross):
    tokens, width = cotangent.shape
    parts = lax.axis_size("wide")
    share = w_cross.shape[1] // parts
    scale = 1.0 / math.sqrt(tokens * parts)
    cuts = row_cuts(tokens)
    n = len(cuts)
    z = n - 1
    end = cuts[z][0]
    far_inputs = swap(saved_inputs, "narrow", 1 << 0)
    saved_inputs, cotangent, w_cross = in_hbm(saved_inputs), in_hbm(cotangent), in_hbm(w_cross)
    chain = Chain()
    near = [[None] * n for _ in range(LEVELS)]
    far = [[None] * n for _ in range(LEVELS)]

    def spread(terms):
        return [terms[0]] + [swap(t, "wide", k) for k, t in enumerate(terms[1:], 1)]

    def send(level, k):
        far[level][k] = [swap(a, "narrow", 1 << level) for a in near[level][k]]

    def flat(arrays):
        return [a for group in arrays for a in group]

    first, cross_1 = cut_out(
        chain,
        [
            [(w_cross, my_share(2), share), (cotangent, rows_at(0), cuts[0][1])],
            [(w_cross, block_of(1), width)],
        ],
        "first_rows",
    )
    cross_1 = swap(cross_1, "narrow", 1 << 1)
    first = swap(first, "narrow", 1 << 2)
    self_2 = weight_sums(
        chain,
        [(saved_inputs, (2,), 0)],
        [[cotangent]],
        [(0, 0)],
        0,
        None,
        scale,
        (1,),
        "self_sums_2",
    )
    self_2 = spread(self_2)
    (self_2,) = add_terms(chain, self_2, "add_self_2", (jnp.float32,))
    starts = cut_out(
        chain, [[(cotangent, rows_at(at), size)] for at, size in cuts[:2]], "rows_0"
    )
    share_2, rows = cut_out(
        chain,
        [[(first, rows_at(0), share)], [(first, rows_at(share), cuts[0][1])]],
        "parted",
        [far_inputs],
    )
    far[2][0], near[2][0] = [rows], [starts[0]]
    near[2][1] = hand_on(chain, [starts[1]], [], "rows_1")
    send(2, 1)
    shares_2 = [(share_2, place_of(0))]
    shares_2 += [(swap(share_2, "wide", k), place_of(k)) for k in range(1, parts)]
    blocks = [None, cross_1, *join_shares(chain, [shares_2], "join_2")]

    def job(level, k):
        return (level, near[level][k][0], far[level][k][0], blocks[level])

    grad = jax.ShapeDtypeStruct((tokens + width, width), cotangent.dtype)

    def level_1(ks, block=None):
        jobs = [job(1, k) for k in ks]
        into = (grad, cuts[ks[0]][0])
        return next_grads(chain, w_self, jobs, f"next_grads_1_{ks[0]}", into, block)

    def sums_a(ks, before, last=None):
        xs = [(saved_inputs, (2,), 0), (saved_inputs, (1,), 0)]
        sides = [flat(far[2][k] for k in ks), flat(near[1][k] for k in ks)]
        start, name = cuts[ks[0]][0], f"sums_a_{ks[0]}"
        return weight_sums(chain, xs, sides, [(0, 0), (1, 1)], start, before, scale, last, name)

    def sums_b(ks, before, last=None):
        xs = [(saved_inputs, (1,), 0), (saved_inputs, (0,), 0), (far_inputs, (0,), 0)]
        pairs = [(0, 0), (1, 1), (2, 1)]
        start, name = cuts[ks[0]][0], f"sums_b_{ks[0]}"
        side = flat(far[1][k] for k in ks)
        return weight_sums(chain, xs, [side, grad], pairs, start, before, scale, last, name)

    def leave(k):
        rows = (cotangent, rows_at(cuts[k][0]), cuts[k][1])
        near[2][k] = cut_out(chain, [[rows]], f"rows_{k}")
        send(2, k)

    sum_a = sum_b = None
    for k in range(n):
        jobs = [job(2, k)] + ([job(1, 0)] if k == 1 else [])
        near[1][k] = next_grads(chain, w_self, jobs, f"next_grads_{k}", (grad, 0) if k == 1 else None)
        if k == 1:
            grad = near[1][k].pop()
        send(1, k)
        if k < 2:
            leave(k + 2)
        if 2 <= k < z - 1:
            (grad,) = level_1([k - 1], (w_cross, 0, tokens) if k == 2 else None)
            leave(k + 2)
        if 1 <= k < z - 1:
            (sum_b,) = sums_b([k - 1], sum_b)
        if 1 <= k < z:
            (sum_a,) = sums_a([0, 1] if k == 1 else [k], sum_a)
    sum_a = spread(sums_a([z], sum_a, (2,)))
    for k in (z - 2, z - 1):
        (grad,) = level_1([k])
        (sum_b,) = sums_b([k], sum_b)
    (grad,) = level_1([z])
    terms = sums_b([z], sum_b, (-1, 2))
    sum_c = spread(terms[parts:])
    cross_2, self_1, grad = add_terms(chain, sum_a, "add_a", (jnp.bfloat16, jnp.float32), grad)
    far_grad = swap(grad, "narrow", 1 << 0)
    cross_1 = [swap_both(terms[0], 0, 1 << 1)]
    cross_2, *terms = hand_on(chain, [cross_2, *terms[1:parts]], [far_grad], "rest")
    cross_1 += [swap_both(t, k, 1 << 1) for k, t in enumerate(terms, 1)]
    cross_2 = swap(cross_2, "narrow", 1 << 2)
    out = last_grad(chain, grad, far_grad, w_self, tokens)
    grad_self, grad_cross = last_sums(chain, cross_1, sum_c, self_1, self_2, cross_2)
    return out, grad_self, grad_cross


def solution(mesh):
    in_specs = (
        P(None, "wide", "narrow"),
        P("wide", "narrow"),
        P(None, "narrow", None),
        P(None, "narrow", None),
    )
    out_specs = (
        P("wide", "narrow"),
        P(None, ("narrow", "wide"), None),
        P(None, ("narrow", "wide"), None),
    )
    return jax.shard_map(local, mesh=mesh, in_specs=in_specs, out_specs=out_specs, check_vma=False)
```
